512 devices in a mesh: ctx: 16 (over z_hi, y), dp: 32 (over z_lo, x, core).
Axes of the slice: x: 4, y: 8, z: 8 (z_hi: 2, z_lo: 4; z = z_hi * 4 + z_lo), core: 2. Of those that a mesh axis runs over, the one named last changes fastest.
Arguments:
- item_first: int32 [32, 2048], P('dp', 'ctx'), may hold values from 0 to 127
- item_second: int32 [32, 2048], P('dp', 'ctx'), may hold values from 0 to 127
- lengths: int32 [32, 2], P('dp'), may hold values from 512 to 1536, as said below
- block_mask: int32 [32, 16, 16], P('dp', 'ctx'), may hold values 0 or 1
- core_first: bfloat16 [128, 1024], P('dp'), may hold values from -6 to 6
- core_second: bfloat16 [128, 1024], P('dp'), may hold values from -1 to 1
- w_proj: bfloat16 [1024, 2048], P(None, 'dp'), may hold values from -0.1875 to 0.1875
- w_out: bfloat16 [512, 1024], P(None, 'dp'), may hold values from -0.25 to 0.25
- cotangent: bfloat16 [32, 2048, 1024], P('dp', 'ctx'), may hold values from -1 to 1
Outputs:
- layer_out: bfloat16 [32, 2048, 1024], P('dp', 'ctx')
- grad_first: float32 [128, 1024], P('dp')
- grad_second: float32 [128, 1024], P('dp')
The draws below stay inside these ranges and needn't reach their ends.
Inputs may be any that keep to these rules, and one draw needn't show every extreme that they name: A pair's two lengths sum to 2048; the first user's events come first.
All inputs are finite; a program needn't handle non-finite values. No bound on the sum of `block_mask` on one device may be relied on, other than what follows from the above.
Results may differ from the reference program's by a relative error of at most 0.022.
Values may be sent and summed in bfloat16 or wider, within the bound.
No kernel may reach another device: no remote copies, remote signals or barrier semaphores. Data moves between devices by JAX's collectives and lax.ppermute only.
A program may use at most 64 MiB of HBM per device.

```python
import math
import jax
import jax.numpy as jnp
import numpy as np
from jax import lax

DA = 32
DB = 32
D = 1024
R = 32
ROWS = 128
H = 4
HD = 128
E = 512
BLK = 128
SEQ = 2048
NBLK = 16
GROUPS = 32


def draw_lengths(key, part):
    key = jax.random.fold_in(key, 5)
    lowest = SEQ - SEQ * 3 // 4
    highest_len = SEQ * 3 // 4
    firsts = jax.random.randint(key, (GROUPS,), lowest, highest_len + 1)
    firsts = firsts.at[0].set(highest_len).at[1].set(lowest)
    return jnp.stack([firsts, SEQ - firsts], axis=1).astype(jnp.int32)


def with_ends(entries, key, smallest, largest):
    longest = entries.shape.index(max(entries.shape))
    spots = []
    for shift in (0, 1):
        where = [jax.random.randint(jax.random.fold_in(key, axis), (), 0, length) for axis, length in enumerate(entries.shape)]
        where[longest] = (where[longest] + shift) % entries.shape[longest]
        spots.append(tuple(where))
    return entries.at[spots[0]].set(smallest).at[spots[1]].set(largest)


def level_of(key, dims, split, low, top_value):
    loudness, own = 1.0, jax.random.fold_in(key, 6)
    for dim, parts in split:
        draws = jnp.exp(jax.random.uniform(jax.random.fold_in(own, dim), (parts,), jnp.float32, low / len(split), top_value / len(split)))
        loudness = loudness * jnp.repeat(draws, dims[dim] // parts).reshape([-1 if axis == dim else 1 for axis in range(len(dims))])
    return loudness


def rank_bounds(number_of, skew):
    portions = [(1 << 20) // math.isqrt(standing ** skew) + 1 for standing in range(1, number_of + 1)]
    scale = 1 + sum(portions) // (1 << 30)
    return np.cumsum(np.array([max(1, weight // scale) for weight in portions]))


def ranked(stream_key, shape, number_of, lean):
    table = rank_bounds(number_of, lean)
    lot = jax.random.randint(jax.random.fold_in(stream_key, 1), shape, 0, int(table[number_of - 1]))
    grade = jnp.searchsorted(jnp.asarray(table, jnp.int32), lot, side="right")
    return jax.random.permutation(jax.random.fold_in(stream_key, 2), number_of)[grade].astype(jnp.int32)


def bell_draw(own_key, dims, deviation, reach, shards=(), kind=jnp.bfloat16):
    entries = deviation * jax.random.normal(own_key, dims, jnp.float32)
    if shards:
        entries = entries * level_of(own_key, dims, shards, -0.22, 0.18)
    return jnp.clip(entries, -reach, reach).astype(kind)


def setup_inputs(seed: int = 0) -> dict:
    key_of = jax.random.split(jax.random.key(seed), 10)
    return {
        "item_first": with_ends(ranked(key_of[0], (GROUPS, SEQ), ROWS, 2), jax.random.fold_in(key_of[0], 3), 0, ROWS - 1).astype(jnp.int32),
        "item_second": with_ends(ranked(key_of[1], (GROUPS, SEQ), ROWS, 2), jax.random.fold_in(key_of[1], 3), 0, ROWS - 1).astype(jnp.int32),
        "lengths": draw_lengths(jax.random.fold_in(key_of[9], 71), 0),
        "block_mask": with_ends((jax.random.randint(key_of[3], (GROUPS, NBLK, NBLK), 0, 4) < 3).astype(jnp.int32), jax.random.fold_in(key_of[3], 1), 0, 1),
        "core_first": bell_draw(key_of[4], (ROWS, DA * R), 1.0, 6.0, ((0, 32),)),
        "core_second": bell_draw(key_of[5], (ROWS, R * DB), R ** -0.5, 1.0, ((0, 32),)),
        "w_proj": bell_draw(key_of[6], (D, 4 * E), D ** -0.5, 0.1875, ((1, 32),)),
        "w_out": bell_draw(key_of[7], (E, D), E ** -0.5, 0.25, ((1, 32),)),
        "cotangent": bell_draw(key_of[8], (GROUPS, SEQ, D), 0.0625, 1.0, ((0, 32), (1, 16))),
    }


epsilon = 1e-05

def normalize(values):
    average = lax.optimization_barrier(jnp.mean(values, axis=-1, keepdims=True))
    centred = values - average
    inv_scale = lax.rsqrt(lax.optimization_barrier(jnp.mean(centred * centred, axis=-1, keepdims=True)) + epsilon)
    return (centred * inv_scale, inv_scale)

def norm_back(upstream, normed, inv_scale):
    return (upstream - lax.optimization_barrier(jnp.mean(upstream, axis=-1, keepdims=True)) - normed * lax.optimization_barrier(jnp.mean(upstream * normed, axis=-1, keepdims=True))) * inv_scale

def silu_slope(values):
    sigmoid_vals = jax.nn.sigmoid(values)
    return sigmoid_vals * (1.0 + values * (1.0 - sigmoid_vals))

def tile_terms(queries, key_rows, query_start, key_start, bitmap, pair_lengths):
    query_count = queries.shape[0]
    key_count = key_rows.shape[0]
    query_heads = queries.astype(jnp.float32).reshape(query_count, H, HD)
    key_heads = key_rows.astype(jnp.float32).reshape(key_count, H, HD)
    scores = jnp.einsum('qhd,khd->hqk', query_heads, key_heads) * HD ** (-0.5)
    query_pos = query_start + jnp.arange(query_count, dtype=jnp.int32)
    key_pos = key_start + jnp.arange(key_count, dtype=jnp.int32)
    query_user = query_pos >= pair_lengths[0]
    key_user = key_pos >= pair_lengths[0]
    block_rows = lax.dynamic_slice(bitmap, (query_start // BLK, key_start // BLK), (query_count // BLK, key_count // BLK))
    block_keep = jnp.repeat(jnp.repeat(block_rows, BLK, axis=0), BLK, axis=1) == 1
    keeping = (key_pos[None, :] >= query_pos[:, None]) & (query_user[:, None] == key_user[None, :]) & block_keep
    user_length = jnp.where(query_user, pair_lengths[1], pair_lengths[0]).astype(jnp.float32)
    scaling = jnp.where(keeping, 1.0 / user_length[:, None], 0.0).astype(jnp.float32)
    sigmoid_vals = jax.nn.sigmoid(scores)
    attention = scores * sigmoid_vals * scaling[None]
    slopes = sigmoid_vals * (1.0 + scores * (1.0 - sigmoid_vals)) * scaling[None]
    return (attention, slopes)

def group_pass(firsts, seconds, pair_lengths, bitmap, upstream, core_first, core_second, w_proj, w_out):
    highest = lax.Precision.HIGHEST
    rows_first = core_first[firsts].astype(jnp.float32).reshape(SEQ, DA, R)
    rows_second = core_second[seconds].astype(jnp.float32).reshape(SEQ, R, DB)
    embedded = jnp.einsum('tar,trb->tab', rows_first, rows_second, precision=highest).reshape(SEQ, D).astype(jnp.bfloat16)
    x_normed, x_scale = normalize(embedded.astype(jnp.float32))
    normed = x_normed.astype(jnp.bfloat16)
    pre_act = jnp.dot(normed, w_proj, preferred_element_type=jnp.float32)
    activated = jax.nn.silu(pre_act).astype(jnp.bfloat16)
    update_gate = activated[:, :E]
    value_rows = activated[:, E:2 * E]
    query_rows = activated[:, 2 * E:3 * E]
    key_rows = activated[:, 3 * E:]
    value_heads = value_rows.astype(jnp.float32).reshape(SEQ, H, HD)
    key_heads = key_rows.astype(jnp.float32).reshape(SEQ, H, HD)
    block_width = 512 if SEQ % 512 == 0 else SEQ
    pieces = []
    for block_index in range(SEQ // block_width):
        lower = block_index * block_width
        attention, unused = tile_terms(query_rows[lower:lower + block_width], key_rows, lower, 0, bitmap, pair_lengths)
        rounded = lax.optimization_barrier(attention.astype(jnp.bfloat16)).astype(jnp.float32)
        pieces.append(jnp.einsum('hqk,khd->qhd', rounded, value_heads))
    mixed = jnp.concatenate(pieces, axis=0).reshape(SEQ, E)
    mixed_normed, mixed_scale = normalize(mixed)
    hidden = (mixed_normed * update_gate.astype(jnp.float32)).astype(jnp.bfloat16)
    layer_out = (embedded.astype(jnp.float32) + jnp.dot(hidden, w_out, preferred_element_type=jnp.float32)).astype(jnp.bfloat16)
    hidden_grad = jnp.dot(upstream, w_out.T, preferred_element_type=jnp.float32)
    gate_grad = hidden_grad * mixed_normed
    mixed_grad = norm_back(hidden_grad * update_gate.astype(jnp.float32), mixed_normed, mixed_scale).astype(jnp.bfloat16)
    grad_heads = mixed_grad.astype(jnp.float32).reshape(SEQ, H, HD)
    query_parts = []
    key_grad = jnp.zeros((SEQ, H, HD), jnp.float32)
    value_grad = jnp.zeros((SEQ, H, HD), jnp.float32)
    for block_index in range(SEQ // block_width):
        lower = block_index * block_width
        query_block = query_rows[lower:lower + block_width].astype(jnp.float32).reshape(block_width, H, HD)
        grad_block = grad_heads[lower:lower + block_width]
        attention, slopes = tile_terms(query_rows[lower:lower + block_width], key_rows, lower, 0, bitmap, pair_lengths)
        rounded = lax.optimization_barrier(attention.astype(jnp.bfloat16)).astype(jnp.float32)
        pressure = jnp.einsum('qhd,khd->hqk', grad_block, value_heads)
        score_grad = lax.optimization_barrier((pressure * slopes).astype(jnp.bfloat16)).astype(jnp.float32)
        query_parts.append(jnp.einsum('hqk,khd->qhd', score_grad, key_heads) * HD ** (-0.5))
        key_grad = key_grad + jnp.einsum('hqk,qhd->khd', score_grad, query_block) * HD ** (-0.5)
        value_grad = value_grad + jnp.einsum('hqk,qhd->khd', rounded, grad_block)
    query_grad = jnp.concatenate(query_parts, axis=0)
    joined = jnp.concatenate([gate_grad, value_grad.reshape(SEQ, E), query_grad.reshape(SEQ, E), key_grad.reshape(SEQ, E)], axis=1)
    pre_grad = (joined * silu_slope(pre_act)).astype(jnp.bfloat16)
    normed_grad = jnp.dot(pre_grad, w_proj.T, preferred_element_type=jnp.float32)
    input_grad = upstream.astype(jnp.float32) + norm_back(normed_grad, x_normed, x_scale)
    embed_grad = input_grad.reshape(SEQ, DA, DB)
    first_terms = jnp.einsum('tab,trb->tar', embed_grad, rows_second, precision=highest).reshape(SEQ, DA * R)
    second_terms = jnp.einsum('tar,tab->trb', rows_first, embed_grad, precision=highest).reshape(SEQ, R * DB)
    first_sum = jax.ops.segment_sum(first_terms, firsts, ROWS)
    second_sum = jax.ops.segment_sum(second_terms, seconds, ROWS)
    return (layer_out, first_sum, second_sum)

def reference(item_first, item_second, lengths, block_mask, core_first, core_second, w_proj, w_out, cotangent):

    def one_group(totals, inputs):
        firsts, seconds, pair_lengths, bitmap, upstream = inputs
        out_rows, first_sum, second_sum = group_pass(firsts, seconds, pair_lengths, bitmap, upstream, core_first, core_second, w_proj, w_out)
        return ((totals[0] + first_sum, totals[1] + second_sum), out_rows)
    initial = (jnp.zeros((ROWS, DA * R), jnp.float32), jnp.zeros((ROWS, R * DB), jnp.float32))
    totals, layer_out = lax.scan(one_group, initial, (item_first, item_second, lengths, block_mask, cotangent))
    return (layer_out, totals[0], totals[1])
```

```python
import jax
import jax.numpy as jnp
from jax import lax
from jax.experimental import pallas as pl
from jax.experimental.pallas import tpu as pltpu
from jax.sharding import PartitionSpec as P

DA = 32
DB = 32
D = 1024
R = 32
ROWS = 128
H = 4
HD = 128
E = 512
BLK = 128
SEQ = 2048
NBLK = 16
TILE = 256
NDP = 32
CHUNK = 512

EPSILON = 1e-05
SCALE = HD ** (-0.5)
F32 = jnp.float32
BF16 = jnp.bfloat16
NT_DIMS = (((1,), (1,)), ((), ()))

SMEM_SPEC = pl.BlockSpec(memory_space=pltpu.SMEM)
VMEM_SPEC = pl.BlockSpec(memory_space=pltpu.VMEM)


def mm(left, right):
    return jnp.dot(left, right, preferred_element_type=F32)


def mm_nt(left, right):
    return lax.dot_general(left, right, NT_DIMS, preferred_element_type=F32)


def sigmoid(values):
    return 0.5 * jnp.tanh(0.5 * values) + 0.5


def silu(values):
    return values * sigmoid(values)


def silu_slope(values):
    sig = sigmoid(values)
    return sig * (1.0 + values * (1.0 - sig))


def flip(values):
    return values.astype(F32).T


def normalize(values, axis):
    average = jnp.mean(values, axis=axis, keepdims=True)
    centred = values - average
    inv_scale = lax.rsqrt(jnp.mean(centred * centred, axis=axis, keepdims=True) + EPSILON)
    return (centred * inv_scale, inv_scale)


def norm_back(upstream, normed, inv_scale):
    return (
        upstream
        - jnp.mean(upstream, axis=-1, keepdims=True)
        - normed * jnp.mean(upstream * normed, axis=-1, keepdims=True)
    ) * inv_scale


def pair_onehot(firsts, seconds):
    row = lax.broadcasted_iota(jnp.int32, (2 * ROWS, BLK), 0)
    core_row = ((row >> 3) << 2) | (row & 3)
    of_first = (row & 4) == 0
    hot_first = jnp.where(of_first & (core_row == firsts), 1.0, 0.0)
    hot_second = jnp.where((~of_first) & (core_row == seconds), 1.0, 0.0)
    return jnp.concatenate([hot_first, hot_second], axis=1).astype(BF16)


def aligned(index, unit):
    return pl.multiple_of(index * unit, unit)


def user_end(last_pos, first_len):
    return jnp.where(last_pos < first_len, first_len, SEQ)


def user_start(first_pos, first_len):
    return jnp.where(first_pos < first_len, 0, first_len)


def up_tiles(pos):
    return (pos + (TILE - 1)) // TILE


def embed_kernel(
    info, indices, table, normed_t, own_terms, own_embedded, table_t, rows_first, rows_second, emb
):
    me = info[0]
    first_len = info[1]
    chunk = me // 4
    low = (user_start(chunk * CHUNK, first_len) // TILE) * 2
    high = up_tiles(user_end(chunk * CHUNK + CHUNK - 1, first_len)) * 2
    for part in range(8):
        table_t[part * 128 : (part + 1) * 128, :] = flip(
            table[:, part * 128 : (part + 1) * 128]
        ).astype(BF16)

    def block(position, carry):
        hot = pair_onehot(indices[position, 0:1, :], indices[position, 1:2, :])
        picked = mm(table_t[...], hot)
        rows_first[...] = picked[:, :BLK]
        rows_second[...] = picked[:, BLK:]

        def group(step, inner):
            base = aligned(step, 128)
            sums = [jnp.zeros((DB, BLK), F32) for _ in range(4)]
            for r in range(R):
                second = rows_second[r * DB : (r + 1) * DB, :]
                for k in range(4):
                    first = rows_first[pl.ds(base + (k * R + r), 1), :]
                    sums[k] = sums[k] + first * second
            for k in range(4):
                emb[pl.ds(pl.multiple_of(base + k * DB, DB), DB), :] = sums[k]
            return inner

        lax.fori_loop(0, 8, group, 0)
        rounded = emb[...].astype(BF16)
        normed, unused = normalize(rounded.astype(F32), 0)
        normed_t[:, pl.ds(aligned(position, BLK), BLK)] = normed.astype(BF16)

        @pl.when(position == me)
        def _():
            own_terms[0] = rows_first[...]
            own_terms[1] = rows_second[...]
            own_embedded[...] = rounded

        return carry

    lax.fori_loop(low, high, block, 0)


def weight_rows(weights, block, first=0, count=8):
    return weights[block * 8 + first : block * 8 + first + count, 0:64, :].reshape(count * 64, D)


def tile_scaling(row_first, column_first, shape, row_is_query, first_len, inverse, keep_low, keep_high):
    rows = row_first + lax.broadcasted_iota(jnp.int32, shape, 0)
    columns = column_first + lax.broadcasted_iota(jnp.int32, shape, 1)
    half = lax.broadcasted_iota(jnp.int32, shape, 1) < BLK
    query, key = (rows, columns) if row_is_query else (columns, rows)
    query_user = (query >= first_len).astype(jnp.int32)
    key_user = (key >= first_len).astype(jnp.int32)
    allowed = jnp.where(half, keep_low, keep_high)
    keep = (key >= query) & (query_user == key_user) & (allowed == 1)
    return jnp.where(keep, jnp.where(query_user == 1, inverse[1], inverse[0]), 0.0)


def forward_kernel(
    info,
    inverse,
    mask,
    normed_t,
    own_embedded,
    weights,
    cotangent,
    layer_out,
    grads_out,
    gate_out,
    keys_head,
    values_head,
    queries_head,
    slopes_out,
    keys_t,
    values_t,
    out_t,
    mixed,
    queries,
):
    me = info[0]
    first_len = info[1]
    chunk = me // 4
    head = me % 4
    kv_low = chunk * 2
    kv_high = up_tiles(user_end(chunk * CHUNK + CHUNK - 1, first_len))
    q_low = user_start(chunk * CHUNK, first_len) // TILE
    q_high = chunk * 2 + 2

    def kv_tile(position, carry):
        columns = pl.ds(aligned(position, TILE), TILE)
        piece = normed_t[:, columns]
        values_t[:, columns] = silu(mm(weight_rows(weights, 1), piece)).astype(BF16)
        keys_t[:, columns] = silu(mm(weight_rows(weights, 3), piece)).astype(BF16)
        return carry

    lax.fori_loop(kv_low, kv_high, kv_tile, 0)
    head_rows = pl.ds(aligned(head, HD), HD)
    keys_head[...] = keys_t[head_rows, :]
    values_head[...] = values_t[head_rows, :]

    def head_weights(block):
        return weights[pl.ds(block * 8 + head * 2, 2), 0:64, :].reshape(HD, D)

    def q_tile(position, carry):
        columns = pl.ds(aligned(position, TILE), TILE)
        queries_head[:, columns] = silu(mm(head_weights(2), normed_t[:, columns])).astype(BF16)
        return carry

    lax.fori_loop(q_low, q_high, q_tile, 0)

    chunk_piece = normed_t[:, pl.ds(aligned(chunk, CHUNK), CHUNK)]
    for place in range(3):
        slopes_out[:, place * HD : (place + 1) * HD] = silu_slope(
            mm(head_weights(place + 1), chunk_piece)
        ).T

    for owner in range(NDP):
        out_t[owner * 32 : owner * 32 + 16, :] = weights[owner, 64:80, :E]
        out_t[owner * 32 + 16 : owner * 32 + 32, :] = weights[owner, 64:80, E:]

    own_normed = flip(normed_t[:, pl.ds(aligned(me, BLK), BLK)]).astype(BF16)
    pre_gate = mm_nt(own_normed, weight_rows(weights, 0))
    gate = silu(pre_gate).astype(BF16).astype(F32)
    queries[...] = silu(mm_nt(own_normed, weight_rows(weights, 2))).astype(BF16)
    mixed[...] = jnp.zeros((BLK, E), F32)

    def attend(position, carry):
        columns = pl.ds(aligned(position, TILE), TILE)
        scaling = tile_scaling(
            me * BLK,
            position * TILE,
            (BLK, TILE),
            True,
            first_len,
            inverse,
            mask[me, position * 2],
            mask[me, position * 2 + 1],
        )
        for h in range(H):
            own = slice(h * HD, (h + 1) * HD)
            scores = mm(queries[:, own], keys_t[own, columns]) * SCALE
            attention = (silu(scores) * scaling).astype(BF16)
            mixed[:, own] += mm_nt(attention, values_t[own, columns])
        return carry

    lax.fori_loop(me // 2, up_tiles(user_end(me * BLK + BLK - 1, first_len)), attend, 0)

    mixed_normed, mixed_scale = normalize(mixed[...], -1)
    hidden = (mixed_normed * gate).astype(BF16)
    layer_out[...] = (flip(own_embedded[...]) + mm_nt(hidden, out_t[...])).astype(BF16)
    hidden_grad = mm(cotangent[...], out_t[...])
    gate_out[...] = (hidden_grad * mixed_normed * silu_slope(pre_gate)).astype(BF16)
    mixed_grad = norm_back(hidden_grad * gate, mixed_normed, mixed_scale).astype(BF16)
    for place in range(NBLK):
        h = place % 4
        grads_out[place] = mixed_grad[:, h * HD : (h + 1) * HD]


def backward_kernel(
    info,
    inverse,
    mask,
    keys_head,
    values_head,
    queries_head,
    grads,
    slopes,
    pre_grads,
    own_keys,
    own_values,
    own_queries,
    sums,
):
    me = info[0]
    first_len = info[1]
    chunk = me // 4
    columns = pl.ds(aligned(chunk, CHUNK), CHUNK)
    own_keys[...] = flip(keys_head[:, columns]).astype(BF16)
    own_values[...] = flip(values_head[:, columns]).astype(BF16)
    own_queries[...] = flip(queries_head[:, columns]).astype(BF16)
    for part in range(4):
        block = chunk * 4 + part
        rows = slice(part * BLK, (part + 1) * BLK)
        sums[...] = jnp.zeros((BLK, 3 * HD), F32)

        def query_side(position, carry):
            tile = pl.ds(aligned(position, TILE), TILE)
            scaling = tile_scaling(
                block * BLK,
                position * TILE,
                (BLK, TILE),
                True,
                first_len,
                inverse,
                mask[block, position * 2],
                mask[block, position * 2 + 1],
            )
            scores = mm(own_queries[rows, :], keys_head[:, tile]) * SCALE
            pressure = mm(grads[pl.ds(aligned(block, BLK), BLK), :], values_head[:, tile])
            score_grad = (pressure * silu_slope(scores) * scaling).astype(BF16)
            sums[:, HD : 2 * HD] += mm_nt(score_grad, keys_head[:, tile])
            return carry

        lax.fori_loop(
            block // 2, up_tiles(user_end(block * BLK + BLK - 1, first_len)), query_side, 0
        )

        def key_side(position, carry):
            tile = pl.ds(aligned(position, TILE), TILE)
            scaling = tile_scaling(
                block * BLK,
                position * TILE,
                (BLK, TILE),
                False,
                first_len,
                inverse,
                mask[position * 2, block],
                mask[position * 2 + 1, block],
            )
            scores = mm(own_keys[rows, :], queries_head[:, tile]) * SCALE
            sig = sigmoid(scores)
            grad_tile = grads[tile, :]
            attention = (scores * sig * scaling).astype(BF16)
            pressure = mm_nt(own_values[rows, :], grad_tile)
            slope = sig * (1.0 + scores * (1.0 - sig))
            score_grad = (pressure * slope * scaling).astype(BF16)
            sums[:, :HD] += mm(attention, grad_tile)
            sums[:, 2 * HD :] += mm_nt(score_grad, queries_head[:, tile])
            return carry

        lax.fori_loop(
            user_start(block * BLK, first_len) // TILE, block // 2 + 1, key_side, 0
        )
        pre_grads[part, :, :HD] = (sums[:, :HD] * slopes[rows, :HD]).astype(BF16)
        pre_grads[part, :, HD:] = (sums[:, HD:] * SCALE * slopes[rows, HD:]).astype(BF16)


def core_kernel(
    gate_grads,
    head_grads,
    weights,
    cotangent,
    own_embedded,
    own_terms,
    indices,
    partial_out,
    rows_second,
    grad_t,
    terms,
):
    normed_grad = mm(gate_grads[...], weight_rows(weights, 0))
    for place in range(3):
        joined = jnp.concatenate(
            [head_grads[h, :, place * HD : (place + 1) * HD] for h in range(H)], axis=1
        )
        normed_grad = normed_grad + mm(joined, weight_rows(weights, place + 1))
    x_normed, x_scale = normalize(flip(own_embedded[...]), -1)
    input_grad = cotangent[...].astype(F32) + norm_back(normed_grad, x_normed, x_scale)
    grad_t[...] = input_grad.T
    for b in range(DB):
        rows_second[b * R : (b + 1) * R, :] = own_terms.at[1][pl.ds(b, R, stride=DB), :]

    def group(step, carry):
        base = aligned(step, 128)
        sums = [jnp.zeros((R, BLK), F32) for _ in range(4)]
        for b in range(DB):
            second = rows_second[b * R : (b + 1) * R, :]
            for k in range(4):
                sums[k] = sums[k] + grad_t[pl.ds(base + (k * DB + b), 1), :] * second
        for k in range(4):
            terms[pl.ds(pl.multiple_of(base + k * R, R), R), :BLK] = sums[k]
        sums = [jnp.zeros((DB, BLK), F32) for _ in range(4)]
        for a in range(DA):
            grad = grad_t[a * DB : (a + 1) * DB, :]
            for k in range(4):
                sums[k] = sums[k] + own_terms[0, pl.ds(a * R + step * 4 + k, 1), :] * grad
        for k in range(4):
            terms[pl.ds(pl.multiple_of(base + k * DB, DB), DB), BLK:] = sums[k]
        return carry

    lax.fori_loop(0, 8, group, 0)
    hot = pair_onehot(indices[0:1, :], indices[1:2, :])
    whole = terms[...]
    upper = whole.astype(BF16)
    lower = (whole - upper.astype(F32)).astype(BF16)
    total = mm_nt(hot, upper) + mm_nt(hot, lower)
    partial_out[...] = total.astype(BF16)


def params(megabytes):
    return pltpu.CompilerParams(vmem_limit_bytes=megabytes * 1024 * 1024)


def shape(dims, kind):
    return jax.ShapeDtypeStruct(dims, kind)


def embed_stage(info, indices, table):
    return pl.pallas_call(
        embed_kernel,
        out_shape=(shape((D, SEQ), BF16), shape((2, D, BLK), F32), shape((D, BLK), BF16)),
        in_specs=[SMEM_SPEC, VMEM_SPEC, VMEM_SPEC],
        out_specs=(VMEM_SPEC,) * 3,
        scratch_shapes=[
            pltpu.VMEM((D, 2 * ROWS), BF16),
            pltpu.VMEM((D, BLK), F32),
            pltpu.VMEM((D, BLK), F32),
            pltpu.VMEM((D, BLK), F32),
        ],
        compiler_params=params(24),
        cost_estimate=pl.CostEstimate(flops=20_000_000_000, bytes_accessed=6_000_000, transcendentals=0),
        name="embed",
    )(info, indices, table)


def forward_stage(info, inverse, mask, normed_t, own_embedded, weights, cotangent):
    return pl.pallas_call(
        forward_kernel,
        out_shape=(
            shape((BLK, D), BF16),
            shape((NBLK, BLK, HD), BF16),
            shape((BLK, E), BF16),
            shape((HD, SEQ), BF16),
            shape((HD, SEQ), BF16),
            shape((HD, SEQ), BF16),
            shape((CHUNK, 3 * HD), F32),
        ),
        in_specs=[SMEM_SPEC] * 3 + [VMEM_SPEC] * 4,
        out_specs=(VMEM_SPEC,) * 7,
        scratch_shapes=[
            pltpu.VMEM((E, SEQ), BF16),
            pltpu.VMEM((E, SEQ), BF16),
            pltpu.VMEM((D, E), BF16),
            pltpu.VMEM((BLK, E), F32),
            pltpu.VMEM((BLK, E), BF16),
        ],
        compiler_params=params(40),
        cost_estimate=pl.CostEstimate(flops=8_000_000_000, bytes_accessed=12_000_000, transcendentals=0),
        name="forward",
    )(info, inverse, mask, normed_t, own_embedded, weights, cotangent)


def backward_stage(info, inverse, mask, keys_head, values_head, queries_head, grads, slopes):
    return pl.pallas_call(
        backward_kernel,
        out_shape=shape((4, BLK, 3 * HD), BF16),
        in_specs=[SMEM_SPEC] * 3 + [VMEM_SPEC] * 5,
        out_specs=VMEM_SPEC,
        scratch_shapes=[pltpu.VMEM((CHUNK, HD), BF16)] * 3 + [pltpu.VMEM((BLK, 3 * HD), F32)],
        compiler_params=params(24),
        name="backward",
    )(info, inverse, mask, keys_head, values_head, queries_head, grads, slopes)


def core_stage(gate_grads, head_grads, weights, cotangent, own_embedded, own_terms, indices):
    return pl.pallas_call(
        core_kernel,
        out_shape=shape((2 * ROWS, D), BF16),
        in_specs=[VMEM_SPEC] * 7,
        out_specs=VMEM_SPEC,
        scratch_shapes=[
            pltpu.VMEM((D, BLK), F32),
            pltpu.VMEM((D, BLK), F32),
            pltpu.VMEM((D, 2 * BLK), F32),
        ],
        compiler_params=params(32),
        name="cores",
    )(gate_grads, head_grads, weights, cotangent, own_embedded, own_terms, indices)


def pack_weights(w_proj, w_out):
    out_t = w_out.T
    return jnp.concatenate([w_proj.T, jnp.concatenate([out_t[:16], out_t[16:]], axis=1)], axis=0)


def pack_indices(item_first, item_second, block_mask):
    mask_row = jnp.pad(block_mask[0], ((0, 0), (0, BLK - NBLK)))
    return jnp.concatenate(
        [item_first, item_second, mask_row, jnp.zeros((5, BLK), jnp.int32)], axis=0
    )


def spread(values, axis, count):
    copies = jnp.broadcast_to(values[None], (count,) + values.shape)
    return lax.all_to_all(copies, axis, 0, 0)


def local(
    item_first, item_second, lengths, block_mask, core_first, core_second, w_proj, w_out, cotangent
):
    me = lax.axis_index("ctx").astype(jnp.int32)
    weights = lax.all_gather(pack_weights(w_proj, w_out), "dp", axis=0, tiled=True)
    weights = weights.reshape(NDP, 80, D)
    table = spread(jnp.concatenate([core_first, core_second], axis=0), "dp", NDP)
    table = table.reshape(2 * ROWS, D)
    own_indices = pack_indices(item_first, item_second, block_mask)
    indices = spread(own_indices, "ctx", NBLK)
    mask = indices[:, 2, :NBLK]
    info = jnp.stack([me, lengths[0, 0], lengths[0, 1], me])
    inverse = 1.0 / lengths[0].astype(F32)
    upstream = cotangent[0]

    normed_t, own_terms, own_embedded = embed_stage(info, indices, table)
    layer_out, grads, gate_grads, keys_head, values_head, queries_head, slopes = forward_stage(
        info, inverse, mask, normed_t, own_embedded, weights, upstream
    )
    grads = lax.all_to_all(grads, "ctx", 0, 0).reshape(SEQ, HD)
    pre_grads = backward_stage(
        info, inverse, mask, keys_head, values_head, queries_head, grads, slopes
    )
    groups = [[4 * c + h for h in range(4)] for c in range(4)]
    head_grads = lax.all_to_all(pre_grads, "ctx", 0, 0, axis_index_groups=groups)
    partial = core_stage(
        gate_grads, head_grads, weights, upstream, own_embedded, own_terms, own_indices
    )
    received = lax.all_to_all(partial.reshape(NDP, 8, D), "dp", 0, 0)
    pair_sum = jnp.sum(received.astype(F32), axis=0)
    total = jnp.sum(spread(pair_sum, "ctx", NBLK), axis=0)
    return (layer_out[None], total[:4], total[4:])


def solution(mesh):
    placed = (
        P("dp", "ctx"),
        P("dp", "ctx"),
        P("dp", None),
        P("dp", "ctx", None),
        P("dp", None),
        P("dp", None),
        P(None, "dp"),
        P(None, "dp"),
        P("dp", "ctx", None),
    )
    return jax.shard_map(
        local,
        mesh=mesh,
        in_specs=placed,
        out_specs=(P("dp", "ctx", None), P("dp", None), P("dp", None)),
        check_vma=False,
    )
```

```python
import jax
import jax.numpy as jnp
from jax import lax
from jax.experimental import pallas as pl
from jax.experimental.pallas import tpu as pltpu
from jax.sharding import PartitionSpec as P

DA = 32
DB = 32
D = 1024
R = 32
ROWS = 128
H = 4
HD = 128
E = 512
BLK = 128
SEQ = 2048
NBLK = 16
TILE = 256
NDP = 32
CHUNK = 512
WIDE = 8

EPSILON = 1e-05
SCALE = HD ** (-0.5)
F32 = jnp.float32
BF16 = jnp.bfloat16
NT_DIMS = (((1,), (1,)), ((), ()))

SMEM_SPEC = pl.BlockSpec(memory_space=pltpu.SMEM)
VMEM_SPEC = pl.BlockSpec(memory_space=pltpu.VMEM)
ANY_SPEC = pl.BlockSpec(memory_space=pl.ANY)


def mm(left, right):
    return jnp.dot(left, right, preferred_element_type=F32)


def mm_nt(left, right):
    return lax.dot_general(left, right, NT_DIMS, preferred_element_type=F32)


def sigmoid(values):
    return 0.5 * jnp.tanh(0.5 * values) + 0.5


def silu(values):
    return values * sigmoid(values)


def silu_slope(values):
    sig = sigmoid(values)
    return sig * (1.0 + values * (1.0 - sig))


def flip(values):
    return values.astype(F32).T


def normalize(values, axis):
    average = jnp.mean(values, axis=axis, keepdims=True)
    centred = values - average
    inv_scale = lax.rsqrt(jnp.mean(centred * centred, axis=axis, keepdims=True) + EPSILON)
    return (centred * inv_scale, inv_scale)


def norm_back(upstream, normed, inv_scale):
    return (
        upstream
        - jnp.mean(upstream, axis=-1, keepdims=True)
        - normed * jnp.mean(upstream * normed, axis=-1, keepdims=True)
    ) * inv_scale


def pair_onehot(firsts, seconds):
    row = lax.broadcasted_iota(jnp.int32, (2 * ROWS, BLK), 0)
    core_row = ((row >> 3) << 2) | (row & 3)
    of_first = (row & 4) == 0
    hot_first = jnp.where(of_first & (core_row == firsts), 1.0, 0.0)
    hot_second = jnp.where((~of_first) & (core_row == seconds), 1.0, 0.0)
    return jnp.concatenate([hot_first, hot_second], axis=1).astype(BF16)


def aligned(index, unit):
    return pl.multiple_of(index * unit, unit)


def user_end(last_pos, first_len):
    return jnp.where(last_pos < first_len, first_len, SEQ)


def user_start(first_pos, first_len):
    return jnp.where(first_pos < first_len, 0, first_len)


def up_tiles(pos):
    return (pos + (TILE - 1)) // TILE


def embed_kernel(
    info, indices, table, normed_t, chunk_terms, chunk_embedded, table_t, rows_first, rows_second, emb
):
    me = info[0]
    first_len = info[1]
    chunk = me // 4
    low = (user_start(chunk * CHUNK, first_len) // TILE) * 2
    high = up_tiles(user_end(chunk * CHUNK + CHUNK - 1, first_len)) * 2
    for part in range(8):
        table_t[part * 128 : (part + 1) * 128, :] = flip(
            table[:, part * 128 : (part + 1) * 128]
        ).astype(BF16)

    def block(position, carry):
        hot = pair_onehot(indices[position, 0:1, :], indices[position, 1:2, :])
        picked = mm(table_t[...], hot)
        rows_first[...] = picked[:, :BLK]
        rows_second[...] = picked[:, BLK:]

        def group(step, inner):
            base = aligned(step, WIDE * 32)
            sums = [jnp.zeros((DB, BLK), F32) for _ in range(WIDE)]
            for r in range(R):
                second = rows_second[r * DB : (r + 1) * DB, :]
                for k in range(WIDE):
                    first = rows_first[pl.ds(base + (k * R + r), 1), :]
                    sums[k] = sums[k] + first * second
            for k in range(WIDE):
                emb[pl.ds(pl.multiple_of(base + k * DB, DB), DB), :] = sums[k]
            return inner

        lax.fori_loop(0, DA // WIDE, group, 0)
        rounded = emb[...].astype(BF16)
        normed, unused = normalize(rounded.astype(F32), 0)
        normed_t[:, pl.ds(aligned(position, BLK), BLK)] = normed.astype(BF16)

        @pl.when(position // 4 == chunk)
        def _():
            place = position % 4
            chunk_terms[place, 0] = rows_first[...]
            chunk_terms[place, 1] = rows_second[...]
            chunk_embedded[place] = rounded

        return carry

    lax.fori_loop(low, high, block, 0)


def weight_rows(weights, block, first=0, count=8):
    return weights[block * 8 + first : block * 8 + first + count, 0:64, :].reshape(count * 64, D)


def tile_scaling(row_first, column_first, shape, row_is_query, first_len, inverse, keep_low, keep_high):
    rows = row_first + lax.broadcasted_iota(jnp.int32, shape, 0)
    columns = column_first + lax.broadcasted_iota(jnp.int32, shape, 1)
    half = lax.broadcasted_iota(jnp.int32, shape, 1) < BLK
    query, key = (rows, columns) if row_is_query else (columns, rows)
    query_user = (query >= first_len).astype(jnp.int32)
    key_user = (key >= first_len).astype(jnp.int32)
    allowed = jnp.where(half, keep_low, keep_high)
    keep = (key >= query) & (query_user == key_user) & (allowed == 1)
    return jnp.where(keep, jnp.where(query_user == 1, inverse[1], inverse[0]), 0.0)


def fetch(source, target, semaphore):
    copy = pltpu.make_async_copy(source, target, semaphore)
    copy.start()
    return copy


def forward_kernel(
    info,
    inverse,
    mask,
    normed_t,
    weights_far,
    cotangent,
    grads_out,
    gate_out,
    hidden_out,
    keys_head,
    values_head,
    out_t,
    weights,
    keys_t,
    values_t,
    mixed,
    queries,
    semaphores,
):
    me = info[0]
    first_len = info[1]
    chunk = me // 4
    head = me % 4
    copies = [
        fetch(
            weights_far.at[pl.ds(block * 8, 8)],
            weights.at[pl.ds(block * 8, 8)],
            semaphores.at[block],
        )
        for block in (1, 3, 0, 2)
    ]
    copies[0].wait()
    copies[1].wait()

    def kv_tile(position, carry):
        columns = pl.ds(aligned(position, TILE), TILE)
        piece = normed_t[:, columns]
        values_t[:, columns] = silu(mm(weight_rows(weights, 1), piece)).astype(BF16)
        keys_t[:, columns] = silu(mm(weight_rows(weights, 3), piece)).astype(BF16)
        return carry

    kv_high = up_tiles(user_end(chunk * CHUNK + CHUNK - 1, first_len))
    lax.fori_loop(chunk * 2, kv_high, kv_tile, 0)
    head_rows = pl.ds(aligned(head, HD), HD)
    keys_head[...] = keys_t[head_rows, :]
    values_head[...] = values_t[head_rows, :]
    copies[2].wait()
    copies[3].wait()

    for owner in range(NDP):
        out_t[owner * 32 : owner * 32 + 16, :] = weights[owner, 64:80, :E]
        out_t[owner * 32 + 16 : owner * 32 + 32, :] = weights[owner, 64:80, E:]

    own_normed = flip(normed_t[:, pl.ds(aligned(me, BLK), BLK)]).astype(BF16)
    pre_gate = mm_nt(own_normed, weight_rows(weights, 0))
    gate = silu(pre_gate).astype(BF16).astype(F32)
    queries[...] = silu(mm_nt(own_normed, weight_rows(weights, 2))).astype(BF16)
    mixed[...] = jnp.zeros((BLK, E), F32)

    def attend(position, carry):
        columns = pl.ds(aligned(position, TILE), TILE)
        scaling = tile_scaling(
            me * BLK,
            position * TILE,
            (BLK, TILE),
            True,
            first_len,
            inverse,
            mask[me, position * 2],
            mask[me, position * 2 + 1],
        )
        for h in range(H):
            own = slice(h * HD, (h + 1) * HD)
            scores = mm(queries[:, own], keys_t[own, columns]) * SCALE
            attention = (silu(scores) * scaling).astype(BF16)
            mixed[:, own] += mm_nt(attention, values_t[own, columns])
        return carry

    lax.fori_loop(me // 2, up_tiles(user_end(me * BLK + BLK - 1, first_len)), attend, 0)

    hidden_grad = mm(cotangent[...], out_t[...])
    mixed_normed, mixed_scale = normalize(mixed[...], -1)
    mixed_grad = norm_back(hidden_grad * gate, mixed_normed, mixed_scale).astype(BF16)
    for place in range(NBLK):
        h = place % 4
        grads_out[place] = mixed_grad[:, h * HD : (h + 1) * HD]
    hidden_out[...] = (mixed_normed * gate).astype(BF16)
    gate_out[...] = (hidden_grad * mixed_normed * silu_slope(pre_gate)).astype(BF16)


def prepare_kernel(
    info,
    normed_t,
    chunk_embedded,
    weights_far,
    hidden,
    out_t,
    keys_head,
    values_head,
    layer_out,
    queries_head,
    slopes_out,
    own_keys,
    own_values,
    own_queries,
    head_weights,
    semaphores,
):
    me = info[0]
    first_len = info[1]
    chunk = me // 4
    head = me % 4
    copies = [
        fetch(
            weights_far.at[pl.ds(block * 8 + head * 2, 2)],
            head_weights.at[block - 1],
            semaphores.at[block - 1],
        )
        for block in (1, 2, 3)
    ]
    layer_out[...] = (flip(chunk_embedded[head]) + mm_nt(hidden[...], out_t[...])).astype(BF16)
    columns = pl.ds(aligned(chunk, CHUNK), CHUNK)
    own_keys[...] = flip(keys_head[:, columns]).astype(BF16)
    own_values[...] = flip(values_head[:, columns]).astype(BF16)
    for copy in copies:
        copy.wait()

    def rows_of(place):
        return head_weights[place, :, 0:64, :].reshape(HD, D)

    def q_tile(position, carry):
        tile = pl.ds(aligned(position, TILE), TILE)
        queries_head[:, tile] = silu(mm(rows_of(1), normed_t[:, tile])).astype(BF16)
        return carry

    lax.fori_loop(user_start(chunk * CHUNK, first_len) // TILE, chunk * 2 + 2, q_tile, 0)
    own_queries[...] = flip(queries_head[:, columns]).astype(BF16)
    chunk_piece = normed_t[:, columns]
    for place in range(3):
        slopes_out[:, place * HD : (place + 1) * HD] = silu_slope(
            mm(rows_of(place), chunk_piece)
        ).T


def backward_kernel(
    info,
    inverse,
    mask,
    indices,
    keys_head,
    values_head,
    queries_head,
    own_keys,
    own_values,
    own_queries,
    grads,
    slopes,
    gate_grads,
    cotangent,
    chunk_embedded,
    chunk_terms,
    weights_far,
    partial_out,
    sums,
    head_weights,
    gate_weights,
    normed_grad,
    grad_t,
    rows_second,
    terms,
    total,
    semaphores,
):
    me = info[0]
    first_len = info[1]
    chunk = me // 4
    head = me % 4
    copies = [
        fetch(
            weights_far.at[pl.ds(block * 8 + head * 2, 2)],
            head_weights.at[block - 1],
            semaphores.at[block],
        )
        for block in (1, 2, 3)
    ] + [fetch(weights_far.at[pl.ds(0, 8)], gate_weights, semaphores.at[0])]
    for copy in copies:
        copy.wait()
    for part in range(4):
        block = chunk * 4 + part
        rows = slice(part * BLK, (part + 1) * BLK)
        sums[...] = jnp.zeros((BLK, 3 * HD), F32)

        def query_side(position, carry):
            tile = pl.ds(aligned(position, TILE), TILE)
            scaling = tile_scaling(
                block * BLK,
                position * TILE,
                (BLK, TILE),
                True,
                first_len,
                inverse,
                mask[block, position * 2],
                mask[block, position * 2 + 1],
            )
            scores = mm(own_queries[rows, :], keys_head[:, tile]) * SCALE
            pressure = mm(grads[pl.ds(aligned(block, BLK), BLK), :], values_head[:, tile])
            score_grad = (pressure * silu_slope(scores) * scaling).astype(BF16)
            sums[:, HD : 2 * HD] += mm_nt(score_grad, keys_head[:, tile])
            return carry

        lax.fori_loop(
            block // 2, up_tiles(user_end(block * BLK + BLK - 1, first_len)), query_side, 0
        )

        def key_side(position, carry):
            tile = pl.ds(aligned(position, TILE), TILE)
            scaling = tile_scaling(
                block * BLK,
                position * TILE,
                (BLK, TILE),
                False,
                first_len,
                inverse,
                mask[position * 2, block],
                mask[position * 2 + 1, block],
            )
            scores = mm(own_keys[rows, :], queries_head[:, tile]) * SCALE
            sig = sigmoid(scores)
            grad_tile = grads[tile, :]
            attention = (scores * sig * scaling).astype(BF16)
            pressure = mm_nt(own_values[rows, :], grad_tile)
            slope = sig * (1.0 + scores * (1.0 - sig))
            score_grad = (pressure * slope * scaling).astype(BF16)
            sums[:, :HD] += mm(attention, grad_tile)
            sums[:, 2 * HD :] += mm_nt(score_grad, queries_head[:, tile])
            return carry

        lax.fori_loop(
            user_start(block * BLK, first_len) // TILE, block // 2 + 1, key_side, 0
        )
        value_pre = (sums[:, :HD] * slopes[rows, :HD]).astype(BF16)
        other_pre = (sums[:, HD:] * SCALE * slopes[rows, HD:]).astype(BF16)
        pre_grad = jnp.concatenate([value_pre, other_pre], axis=1)
        normed_grad[...] = mm(pre_grad, head_weights[:, :, 0:64, :].reshape(3 * HD, D))

        @pl.when(head == part)
        def _():
            normed_grad[...] += mm(gate_grads[...], gate_weights[:, 0:64, :].reshape(E, D))

        x_normed, x_scale = normalize(chunk_embedded[part].astype(F32), 0)
        upstream = normed_grad[...].T
        grad_t[...] = (
            upstream
            - jnp.mean(upstream, axis=0, keepdims=True)
            - x_normed * jnp.mean(upstream * x_normed, axis=0, keepdims=True)
        ) * x_scale

        @pl.when(head == part)
        def _():
            grad_t[...] += flip(cotangent[...])

        for b in range(DB):
            rows_second[b * R : (b + 1) * R, :] = chunk_terms.at[part, 1][pl.ds(b, R, stride=DB), :]

        def group(step, carry):
            base = aligned(step, WIDE * 32)
            sums = [jnp.zeros((R, BLK), F32) for _ in range(WIDE)]
            for b in range(DB):
                second = rows_second[b * R : (b + 1) * R, :]
                for k in range(WIDE):
                    sums[k] = sums[k] + grad_t[pl.ds(base + (k * DB + b), 1), :] * second
            for k in range(WIDE):
                terms[pl.ds(pl.multiple_of(base + k * R, R), R), :BLK] = sums[k]
            sums = [jnp.zeros((DB, BLK), F32) for _ in range(WIDE)]
            for a in range(DA):
                grad = grad_t[a * DB : (a + 1) * DB, :]
                for k in range(WIDE):
                    first = chunk_terms[part, 0, pl.ds(a * R + step * WIDE + k, 1), :]
                    sums[k] = sums[k] + first * grad
            for k in range(WIDE):
                terms[pl.ds(pl.multiple_of(base + k * DB, DB), DB), BLK:] = sums[k]
            return carry

        lax.fori_loop(0, DA // WIDE, group, 0)
        hot = pair_onehot(indices[block, 0:1, :], indices[block, 1:2, :])
        whole = terms[...]
        upper = whole.astype(BF16)
        lower = (whole - upper.astype(F32)).astype(BF16)
        added = mm_nt(hot, upper) + mm_nt(hot, lower)
        if part == 0:
            total[...] = added
        elif part < 3:
            total[...] += added
        else:
            partial_out[...] = (total[...] + added).astype(BF16)


def params(megabytes):
    return pltpu.CompilerParams(vmem_limit_bytes=megabytes * 1024 * 1024)


def shape(dims, kind):
    return jax.ShapeDtypeStruct(dims, kind)


def cost(flops, moved):
    return pl.CostEstimate(flops=flops, bytes_accessed=moved, transcendentals=0)


def embed_stage(info, indices, table):
    return pl.pallas_call(
        embed_kernel,
        out_shape=(
            shape((D, SEQ), BF16),
            shape((4, 2, D, BLK), F32),
            shape((4, D, BLK), BF16),
        ),
        in_specs=[SMEM_SPEC, VMEM_SPEC, VMEM_SPEC],
        out_specs=(VMEM_SPEC,) * 3,
        scratch_shapes=[
            pltpu.VMEM((D, 2 * ROWS), BF16),
            pltpu.VMEM((D, BLK), F32),
            pltpu.VMEM((D, BLK), F32),
            pltpu.VMEM((D, BLK), F32),
        ],
        compiler_params=params(20),
        cost_estimate=cost(20_000_000_000, 6_000_000),
        name="embed",
    )(info, indices, table)


def forward_stage(info, inverse, mask, normed_t, weights, cotangent):
    return pl.pallas_call(
        forward_kernel,
        out_shape=(
            shape((NBLK, BLK, HD), BF16),
            shape((BLK, E), BF16),
            shape((BLK, E), BF16),
            shape((HD, SEQ), BF16),
            shape((HD, SEQ), BF16),
            shape((D, E), BF16),
        ),
        in_specs=[SMEM_SPEC] * 3 + [VMEM_SPEC, ANY_SPEC, VMEM_SPEC],
        out_specs=(VMEM_SPEC,) * 6,
        scratch_shapes=[
            pltpu.VMEM((NDP, 80, D), BF16),
            pltpu.VMEM((E, SEQ), BF16),
            pltpu.VMEM((E, SEQ), BF16),
            pltpu.VMEM((BLK, E), F32),
            pltpu.VMEM((BLK, E), BF16),
            pltpu.SemaphoreType.DMA((4,)),
        ],
        compiler_params=params(24),
        cost_estimate=cost(8_000_000_000, 12_000_000),
        name="forward",
    )(info, inverse, mask, normed_t, weights, cotangent)


def prepare_stage(info, normed_t, chunk_embedded, weights, hidden, out_t, keys_head, values_head):
    return pl.pallas_call(
        prepare_kernel,
        out_shape=(
            shape((BLK, D), BF16),
            shape((HD, SEQ), BF16),
            shape((CHUNK, 3 * HD), F32),
            shape((CHUNK, HD), BF16),
            shape((CHUNK, HD), BF16),
            shape((CHUNK, HD), BF16),
        ),
        in_specs=[SMEM_SPEC, VMEM_SPEC, VMEM_SPEC, ANY_SPEC] + [VMEM_SPEC] * 4,
        out_specs=(VMEM_SPEC,) * 6,
        scratch_shapes=[
            pltpu.VMEM((3, 2, 80, D), BF16),
            pltpu.SemaphoreType.DMA((3,)),
        ],
        compiler_params=params(20),
        cost_estimate=cost(3_000_000_000, 6_000_000),
        name="prepare",
    )(info, normed_t, chunk_embedded, weights, hidden, out_t, keys_head, values_head)


def backward_stage(info, inverse, mask, *arrays):
    return pl.pallas_call(
        backward_kernel,
        out_shape=shape((2 * ROWS, D), BF16),
        in_specs=[SMEM_SPEC] * 3 + [VMEM_SPEC] * 13 + [ANY_SPEC],
        out_specs=VMEM_SPEC,
        scratch_shapes=[
            pltpu.VMEM((BLK, 3 * HD), F32),
            pltpu.VMEM((3, 2, 80, D), BF16),
            pltpu.VMEM((8, 80, D), BF16),
            pltpu.VMEM((BLK, D), F32),
            pltpu.VMEM((D, BLK), F32),
            pltpu.VMEM((D, BLK), F32),
            pltpu.VMEM((D, 2 * BLK), F32),
            pltpu.VMEM((2 * ROWS, D), F32),
            pltpu.SemaphoreType.DMA((4,)),
        ],
        compiler_params=params(28),
        cost_estimate=cost(10_000_000_000, 12_000_000),
        name="backward",
    )(info, inverse, mask, *arrays)


def pack_weights(w_proj, w_out):
    out_t = w_out.T
    return jnp.concatenate([w_proj.T, jnp.concatenate([out_t[:16], out_t[16:]], axis=1)], axis=0)


def pack_indices(item_first, item_second, block_mask):
    mask_row = jnp.pad(block_mask[0], ((0, 0), (0, BLK - NBLK)))
    return jnp.concatenate(
        [item_first, item_second, mask_row, jnp.zeros((5, BLK), jnp.int32)], axis=0
    )


def exchange(values, axis, groups=None):
    return lax.all_to_all(values, axis, 0, 0, axis_index_groups=groups)


def spread(values, axis, count, groups=None):
    return exchange(jnp.broadcast_to(values[None], (count,) + values.shape), axis, groups)


NEAR = [[4 * c + h for h in range(4)] for c in range(4)]
FAR = [[4 * c + h for c in range(4)] for h in range(4)]


def local(
    item_first, item_second, lengths, block_mask, core_first, core_second, w_proj, w_out, cotangent
):
    me = lax.axis_index("ctx").astype(jnp.int32)
    weights = lax.all_gather(pack_weights(w_proj, w_out), "dp", axis=0, tiled=True)
    weights = weights.reshape(NDP, 80, D)
    table = spread(jnp.concatenate([core_first, core_second], axis=0), "dp", NDP)
    table = table.reshape(2 * ROWS, D)
    own_indices = pack_indices(item_first, item_second, block_mask)
    near_indices = spread(own_indices, "ctx", 4, NEAR)
    indices = spread(near_indices, "ctx", 4, FAR).reshape(NBLK, 8, BLK)
    mask = indices[:, 2, :NBLK]
    info = jnp.stack([me, lengths[0, 0], lengths[0, 1], me])
    inverse = 1.0 / lengths[0].astype(F32)
    upstream = cotangent[0]

    normed_t, chunk_terms, chunk_embedded = embed_stage(info, indices, table)
    grads, gate_grads, hidden, keys_head, values_head, out_t = forward_stage(
        info, inverse, mask, normed_t, weights, upstream
    )
    grads = exchange(grads, "ctx").reshape(SEQ, HD)
    layer_out, queries_head, slopes, own_keys, own_values, own_queries = prepare_stage(
        info, normed_t, chunk_embedded, weights, hidden, out_t, keys_head, values_head
    )
    partial = backward_stage(
        info,
        inverse,
        mask,
        indices,
        keys_head,
        values_head,
        queries_head,
        own_keys,
        own_values,
        own_queries,
        grads,
        slopes,
        gate_grads,
        upstream,
        chunk_embedded,
        chunk_terms,
        weights,
    )
    received = exchange(partial.reshape(NDP, 8, D), "dp")
    pair_sum = jnp.sum(received.astype(F32), axis=0).astype(BF16)
    total = jnp.sum(spread(pair_sum, "ctx", NBLK).astype(F32), axis=0)
    return (layer_out[None], total[:4], total[4:])


def solution(mesh):
    placed = (
        P("dp", "ctx"),
        P("dp", "ctx"),
        P("dp", None),
        P("dp", "ctx", None),
        P("dp", None),
        P("dp", None),
        P(None, "dp"),
        P(None, "dp"),
        P("dp", "ctx", None),
    )
    return jax.shard_map(
        local,
        mesh=mesh,
        in_specs=placed,
        out_specs=(P("dp", "ctx", None), P("dp", None), P("dp", None)),
        check_vma=False,
    )
```

```python
import jax
import jax.numpy as jnp
from jax import lax
from jax.experimental import pallas as pl
from jax.experimental.pallas import tpu as pltpu
from jax.sharding import PartitionSpec as P

DA = 32
DB = 32
D = 1024
R = 32
ROWS = 128
H = 4
HD = 128
E = 512
BLK = 128
SEQ = 2048
NBLK = 16
TILE = 256
NDP = 32
CHUNK = 512
WIDE = 8

EPSILON = 1e-05
SCALE = HD ** (-0.5)
F32 = jnp.float32
BF16 = jnp.bfloat16
NT_DIMS = (((1,), (1,)), ((), ()))

SMEM_SPEC = pl.BlockSpec(memory_space=pltpu.SMEM)
VMEM_SPEC = pl.BlockSpec(memory_space=pltpu.VMEM)
HBM_SPEC = pl.BlockSpec(memory_space=pltpu.HBM)


def mm(left, right):
    return jnp.dot(left, right, preferred_element_type=F32)


def mm_nt(left, right):
    return lax.dot_general(left, right, NT_DIMS, preferred_element_type=F32)


def sigmoid(values):
    return 0.5 * jnp.tanh(0.5 * values) + 0.5


def silu(values):
    return values * sigmoid(values)


def silu_slope(values):
    sig = sigmoid(values)
    return sig * (1.0 + values * (1.0 - sig))


def flip(values):
    return values.astype(F32).T


def normalize(values, axis):
    average = jnp.mean(values, axis=axis, keepdims=True)
    centred = values - average
    inv_scale = lax.rsqrt(jnp.mean(centred * centred, axis=axis, keepdims=True) + EPSILON)
    return (centred * inv_scale, inv_scale)


def norm_back(upstream, normed, inv_scale):
    return (
        upstream
        - jnp.mean(upstream, axis=-1, keepdims=True)
        - normed * jnp.mean(upstream * normed, axis=-1, keepdims=True)
    ) * inv_scale


def pair_onehot(firsts, seconds):
    row = lax.broadcasted_iota(jnp.int32, (2 * ROWS, BLK), 0)
    core_row = ((row >> 3) << 2) | (row & 3)
    of_first = (row & 4) == 0
    hot_first = jnp.where(of_first & (core_row == firsts), 1.0, 0.0)
    hot_second = jnp.where((~of_first) & (core_row == seconds), 1.0, 0.0)
    return jnp.concatenate([hot_first, hot_second], axis=1).astype(BF16)


def aligned(index, unit):
    return pl.multiple_of(index * unit, unit)


def user_end(last_pos, first_len):
    return jnp.where(last_pos < first_len, first_len, SEQ)


def user_start(first_pos, first_len):
    return jnp.where(first_pos < first_len, 0, first_len)


def up_tiles(pos):
    return (pos + (TILE - 1)) // TILE


def embed_kernel(
    info,
    indices,
    table,
    normed_far,
    own_terms,
    own_embedded,
    table_t,
    rows_first,
    rows_second,
    emb,
    normed_t,
    semaphores,
):
    me = info[0]
    first_len = info[1]
    chunk = me // 4
    low = (user_start(chunk * CHUNK, first_len) // TILE) * 2
    high = up_tiles(user_end(chunk * CHUNK + CHUNK - 1, first_len)) * 2
    for part in range(8):
        table_t[part * 128 : (part + 1) * 128, :] = flip(
            table[:, part * 128 : (part + 1) * 128]
        ).astype(BF16)

    def send(position):
        columns = pl.ds(aligned(position, BLK), BLK)
        return pltpu.make_async_copy(
            normed_t.at[:, columns], normed_far.at[:, columns], semaphores.at[position]
        )

    def block(position, carry):
        hot = pair_onehot(indices[position, 0:1, :], indices[position, 1:2, :])
        picked = mm(table_t[...], hot)
        rows_first[...] = picked[:, :BLK]
        rows_second[...] = picked[:, BLK:]

        def group(step, inner):
            base = aligned(step, WIDE * 32)
            sums = [jnp.zeros((DB, BLK), F32) for _ in range(WIDE)]
            for r in range(R):
                second = rows_second[r * DB : (r + 1) * DB, :]
                for k in range(WIDE):
                    first = rows_first[pl.ds(base + (k * R + r), 1), :]
                    sums[k] = sums[k] + first * second
            for k in range(WIDE):
                emb[pl.ds(pl.multiple_of(base + k * DB, DB), DB), :] = sums[k]
            return inner

        lax.fori_loop(0, DA // WIDE, group, 0)
        rounded = emb[...].astype(BF16)
        normed, unused = normalize(rounded.astype(F32), 0)
        normed_t[:, pl.ds(aligned(position, BLK), BLK)] = normed.astype(BF16)
        send(position).start()

        @pl.when(position == me)
        def _():
            own_terms[0] = rows_first[...]
            own_terms[1] = rows_second[...]
            own_embedded[...] = rounded

        return carry

    def finish(position, carry):
        send(position).wait()
        return carry

    lax.fori_loop(low, high, block, 0)
    lax.fori_loop(low, high, finish, 0)


def weight_rows(weights, block, first=0, count=8):
    return weights[block * 8 + first : block * 8 + first + count, 0:64, :].reshape(count * 64, D)


def tile_scaling(row_first, column_first, shape, row_is_query, first_len, inverse, keep_low, keep_high):
    rows = row_first + lax.broadcasted_iota(jnp.int32, shape, 0)
    columns = column_first + lax.broadcasted_iota(jnp.int32, shape, 1)
    half = lax.broadcasted_iota(jnp.int32, shape, 1) < BLK
    query, key = (rows, columns) if row_is_query else (columns, rows)
    query_user = (query >= first_len).astype(jnp.int32)
    key_user = (key >= first_len).astype(jnp.int32)
    allowed = jnp.where(half, keep_low, keep_high)
    keep = (key >= query) & (query_user == key_user) & (allowed == 1)
    return jnp.where(keep, jnp.where(query_user == 1, inverse[1], inverse[0]), 0.0)


def fetch(source, target, semaphore):
    copy = pltpu.make_async_copy(source, target, semaphore)
    copy.start()
    return copy


def fetch_weights(far, near, semaphores, order):
    parts = [pl.ds(block * 8, 8) for block in order]
    return [
        fetch(far.at[part], near.at[part], semaphores.at[place])
        for place, part in enumerate(parts)
    ]


def forward_kernel(
    info,
    inverse,
    mask,
    normed_far,
    own_embedded,
    weights_far,
    cotangent,
    layer_out,
    grads_out,
    gate_out,
    keys_head,
    values_head,
    queries_head,
    slopes_out,
    keys_t,
    values_t,
    out_t,
    mixed,
    queries,
    weights,
    normed_t,
    semaphores,
    tile_semaphores,
):
    copies = fetch_weights(weights_far, weights, semaphores, (1, 3, 2, 0))
    me = info[0]
    first_len = info[1]
    chunk = me // 4
    head = me % 4
    kv_low = chunk * 2
    kv_high = up_tiles(user_end(chunk * CHUNK + CHUNK - 1, first_len))
    q_low = user_start(chunk * CHUNK, first_len) // TILE
    q_high = chunk * 2 + 2


    def receive(position):
        columns = pl.ds(aligned(position, TILE), TILE)
        return pltpu.make_async_copy(
            normed_far.at[:, columns], normed_t.at[:, columns], tile_semaphores.at[position]
        )

    def begin(position, carry):
        receive(position).start()
        return carry

    def finish(position, carry):
        receive(position).wait()
        return carry

    lax.fori_loop(kv_low, kv_high, begin, 0)
    lax.fori_loop(q_low, kv_low, begin, 0)
    copies[0].wait()
    copies[1].wait()

    def kv_tile(position, carry):
        columns = pl.ds(aligned(position, TILE), TILE)
        receive(position).wait()
        piece = normed_t[:, columns]
        values_t[:, columns] = silu(mm(weight_rows(weights, 1), piece)).astype(BF16)
        keys_t[:, columns] = silu(mm(weight_rows(weights, 3), piece)).astype(BF16)
        return carry

    lax.fori_loop(kv_low, kv_high, kv_tile, 0)
    head_rows = pl.ds(aligned(head, HD), HD)
    keys_head[...] = keys_t[head_rows, :]
    values_head[...] = values_t[head_rows, :]

    lax.fori_loop(q_low, kv_low, finish, 0)
    copies[2].wait()
    copies[3].wait()

    def head_weights(block):
        return weights[pl.ds(block * 8 + head * 2, 2), 0:64, :].reshape(HD, D)

    def q_tile(position, carry):
        columns = pl.ds(aligned(position, TILE), TILE)
        queries_head[:, columns] = silu(mm(head_weights(2), normed_t[:, columns])).astype(BF16)
        return carry

    lax.fori_loop(q_low, q_high, q_tile, 0)

    chunk_piece = normed_t[:, pl.ds(aligned(chunk, CHUNK), CHUNK)]
    for place in range(3):
        slopes_out[:, place * HD : (place + 1) * HD] = silu_slope(
            mm(head_weights(place + 1), chunk_piece)
        ).T

    for owner in range(NDP):
        out_t[owner * 32 : owner * 32 + 16, :] = weights[owner, 64:80, :E]
        out_t[owner * 32 + 16 : owner * 32 + 32, :] = weights[owner, 64:80, E:]

    own_normed = flip(normed_t[:, pl.ds(aligned(me, BLK), BLK)]).astype(BF16)
    pre_gate = mm_nt(own_normed, weight_rows(weights, 0))
    gate = silu(pre_gate).astype(BF16).astype(F32)
    queries[...] = silu(mm_nt(own_normed, weight_rows(weights, 2))).astype(BF16)
    mixed[...] = jnp.zeros((BLK, E), F32)

    def attend(position, carry):
        columns = pl.ds(aligned(position, TILE), TILE)
        scaling = tile_scaling(
            me * BLK,
            position * TILE,
            (BLK, TILE),
            True,
            first_len,
            inverse,
            mask[me, position * 2],
            mask[me, position * 2 + 1],
        )
        for h in range(H):
            own = slice(h * HD, (h + 1) * HD)
            scores = mm(queries[:, own], keys_t[own, columns]) * SCALE
            attention = (silu(scores) * scaling).astype(BF16)
            mixed[:, own] += mm_nt(attention, values_t[own, columns])
        return carry

    lax.fori_loop(me // 2, up_tiles(user_end(me * BLK + BLK - 1, first_len)), attend, 0)

    mixed_normed, mixed_scale = normalize(mixed[...], -1)
    hidden = (mixed_normed * gate).astype(BF16)
    layer_out[...] = (flip(own_embedded[...]) + mm_nt(hidden, out_t[...])).astype(BF16)
    hidden_grad = mm(cotangent[...], out_t[...])
    gate_out[...] = (hidden_grad * mixed_normed * silu_slope(pre_gate)).astype(BF16)
    mixed_grad = norm_back(hidden_grad * gate, mixed_normed, mixed_scale).astype(BF16)
    for place in range(NBLK):
        h = place % 4
        grads_out[place] = mixed_grad[:, h * HD : (h + 1) * HD]


def backward_kernel(
    info,
    inverse,
    mask,
    keys_head,
    values_head,
    queries_head,
    grads,
    slopes,
    pre_grads,
    own_keys,
    own_values,
    own_queries,
    sums,
):
    me = info[0]
    first_len = info[1]
    chunk = me // 4
    columns = pl.ds(aligned(chunk, CHUNK), CHUNK)
    own_keys[...] = flip(keys_head[:, columns]).astype(BF16)
    own_values[...] = flip(values_head[:, columns]).astype(BF16)
    own_queries[...] = flip(queries_head[:, columns]).astype(BF16)
    for part in range(4):
        block = chunk * 4 + part
        rows = slice(part * BLK, (part + 1) * BLK)
        sums[...] = jnp.zeros((BLK, 3 * HD), F32)

        def query_side(position, carry):
            tile = pl.ds(aligned(position, TILE), TILE)
            scaling = tile_scaling(
                block * BLK,
                position * TILE,
                (BLK, TILE),
                True,
                first_len,
                inverse,
                mask[block, position * 2],
                mask[block, position * 2 + 1],
            )
            scores = mm(own_queries[rows, :], keys_head[:, tile]) * SCALE
            pressure = mm(grads[pl.ds(aligned(block, BLK), BLK), :], values_head[:, tile])
            score_grad = (pressure * silu_slope(scores) * scaling).astype(BF16)
            sums[:, HD : 2 * HD] += mm_nt(score_grad, keys_head[:, tile])
            return carry

        lax.fori_loop(
            block // 2, up_tiles(user_end(block * BLK + BLK - 1, first_len)), query_side, 0
        )

        def key_side(position, carry):
            tile = pl.ds(aligned(position, TILE), TILE)
            scaling = tile_scaling(
                block * BLK,
                position * TILE,
                (BLK, TILE),
                False,
                first_len,
                inverse,
                mask[position * 2, block],
                mask[position * 2 + 1, block],
            )
            scores = mm(own_keys[rows, :], queries_head[:, tile]) * SCALE
            sig = sigmoid(scores)
            grad_tile = grads[tile, :]
            attention = (scores * sig * scaling).astype(BF16)
            pressure = mm_nt(own_values[rows, :], grad_tile)
            slope = sig * (1.0 + scores * (1.0 - sig))
            score_grad = (pressure * slope * scaling).astype(BF16)
            sums[:, :HD] += mm(attention, grad_tile)
            sums[:, 2 * HD :] += mm_nt(score_grad, queries_head[:, tile])
            return carry

        lax.fori_loop(
            user_start(block * BLK, first_len) // TILE, block // 2 + 1, key_side, 0
        )
        pre_grads[part, :, :HD] = (sums[:, :HD] * slopes[rows, :HD]).astype(BF16)
        pre_grads[part, :, HD:] = (sums[:, HD:] * SCALE * slopes[rows, HD:]).astype(BF16)


def core_kernel(
    gate_grads,
    head_grads,
    weights_far,
    cotangent,
    own_embedded,
    own_terms,
    indices,
    partial_out,
    rows_second,
    grad_t,
    terms,
    weights,
    semaphores,
):
    copies = fetch_weights(weights_far, weights, semaphores, (0, 1, 2, 3))
    x_normed, x_scale = normalize(flip(own_embedded[...]), -1)
    copies[0].wait()
    normed_grad = mm(gate_grads[...], weight_rows(weights, 0))
    for place in range(3):
        copies[place + 1].wait()
        joined = jnp.concatenate(
            [head_grads[h, :, place * HD : (place + 1) * HD] for h in range(H)], axis=1
        )
        normed_grad = normed_grad + mm(joined, weight_rows(weights, place + 1))
    input_grad = cotangent[...].astype(F32) + norm_back(normed_grad, x_normed, x_scale)
    grad_t[...] = input_grad.T
    for b in range(DB):
        rows_second[b * R : (b + 1) * R, :] = own_terms.at[1][pl.ds(b, R, stride=DB), :]

    def group(step, carry):
        base = aligned(step, WIDE * 32)
        sums = [jnp.zeros((R, BLK), F32) for _ in range(WIDE)]
        for b in range(DB):
            second = rows_second[b * R : (b + 1) * R, :]
            for k in range(WIDE):
                sums[k] = sums[k] + grad_t[pl.ds(base + (k * DB + b), 1), :] * second
        for k in range(WIDE):
            terms[pl.ds(pl.multiple_of(base + k * R, R), R), :BLK] = sums[k]
        sums = [jnp.zeros((DB, BLK), F32) for _ in range(WIDE)]
        for a in range(DA):
            grad = grad_t[a * DB : (a + 1) * DB, :]
            for k in range(WIDE):
                first = own_terms[0, pl.ds(a * R + step * WIDE + k, 1), :]
                sums[k] = sums[k] + first * grad
        for k in range(WIDE):
            terms[pl.ds(pl.multiple_of(base + k * DB, DB), DB), BLK:] = sums[k]
        return carry

    lax.fori_loop(0, DA // WIDE, group, 0)
    hot = pair_onehot(indices[0:1, :], indices[1:2, :])
    whole = terms[...]
    upper = whole.astype(BF16)
    lower = (whole - upper.astype(F32)).astype(BF16)
    total = mm_nt(hot, upper) + mm_nt(hot, lower)
    partial_out[...] = total.astype(BF16)


def params(megabytes):
    return pltpu.CompilerParams(vmem_limit_bytes=megabytes * 1024 * 1024)


def shape(dims, kind):
    return jax.ShapeDtypeStruct(dims, kind)


def embed_stage(info, indices, table):
    return pl.pallas_call(
        embed_kernel,
        out_shape=(shape((D, SEQ), BF16), shape((2, D, BLK), F32), shape((D, BLK), BF16)),
        in_specs=[SMEM_SPEC, VMEM_SPEC, VMEM_SPEC],
        out_specs=(HBM_SPEC, VMEM_SPEC, VMEM_SPEC),
        scratch_shapes=[
            pltpu.VMEM((D, 2 * ROWS), BF16),
            pltpu.VMEM((D, BLK), F32),
            pltpu.VMEM((D, BLK), F32),
            pltpu.VMEM((D, BLK), F32),
            pltpu.VMEM((D, SEQ), BF16),
            pltpu.SemaphoreType.DMA((NBLK,)),
        ],
        compiler_params=params(57),
        cost_estimate=pl.CostEstimate(flops=20_000_000_000, bytes_accessed=6_000_000, transcendentals=0),
        name="embed",
    )(info, indices, table)


def forward_stage(info, inverse, mask, normed_t, own_embedded, weights, cotangent):
    return pl.pallas_call(
        forward_kernel,
        out_shape=(
            shape((BLK, D), BF16),
            shape((NBLK, BLK, HD), BF16),
            shape((BLK, E), BF16),
            shape((HD, SEQ), BF16),
            shape((HD, SEQ), BF16),
            shape((HD, SEQ), BF16),
            shape((CHUNK, 3 * HD), F32),
        ),
        in_specs=[SMEM_SPEC] * 3 + [HBM_SPEC, VMEM_SPEC, HBM_SPEC, VMEM_SPEC],
        out_specs=(VMEM_SPEC,) * 7,
        scratch_shapes=[
            pltpu.VMEM((E, SEQ), BF16),
            pltpu.VMEM((E, SEQ), BF16),
            pltpu.VMEM((D, E), BF16),
            pltpu.VMEM((BLK, E), F32),
            pltpu.VMEM((BLK, E), BF16),
            pltpu.VMEM((NDP, 80, D), BF16),
            pltpu.VMEM((D, SEQ), BF16),
            pltpu.SemaphoreType.DMA((4,)),
            pltpu.SemaphoreType.DMA((8,)),
        ],
        compiler_params=params(50),
        cost_estimate=pl.CostEstimate(flops=8_000_000_000, bytes_accessed=12_000_000, transcendentals=0),
        name="forward",
    )(info, inverse, mask, normed_t, own_embedded, weights, cotangent)


def backward_stage(info, inverse, mask, keys_head, values_head, queries_head, grads, slopes):
    return pl.pallas_call(
        backward_kernel,
        out_shape=shape((4, BLK, 3 * HD), BF16),
        in_specs=[SMEM_SPEC] * 3 + [VMEM_SPEC] * 5,
        out_specs=VMEM_SPEC,
        scratch_shapes=[pltpu.VMEM((CHUNK, HD), BF16)] * 3 + [pltpu.VMEM((BLK, 3 * HD), F32)],
        compiler_params=params(16),
        name="backward",
    )(info, inverse, mask, keys_head, values_head, queries_head, grads, slopes)


def core_stage(gate_grads, head_grads, weights, cotangent, own_embedded, own_terms, indices):
    return pl.pallas_call(
        core_kernel,
        out_shape=shape((2 * ROWS, D), BF16),
        in_specs=[VMEM_SPEC, VMEM_SPEC, HBM_SPEC] + [VMEM_SPEC] * 4,
        out_specs=VMEM_SPEC,
        scratch_shapes=[
            pltpu.VMEM((D, BLK), F32),
            pltpu.VMEM((D, BLK), F32),
            pltpu.VMEM((D, 2 * BLK), F32),
            pltpu.VMEM((NDP, 80, D), BF16),
            pltpu.SemaphoreType.DMA((4,)),
        ],
        compiler_params=params(50),
        name="cores",
    )(gate_grads, head_grads, weights, cotangent, own_embedded, own_terms, indices)


def pack_weights(w_proj, w_out):
    out_t = w_out.T
    return jnp.concatenate([w_proj.T, jnp.concatenate([out_t[:16], out_t[16:]], axis=1)], axis=0)


def pack_indices(item_first, item_second, block_mask):
    mask_row = jnp.pad(block_mask[0], ((0, 0), (0, BLK - NBLK)))
    return jnp.concatenate(
        [item_first, item_second, mask_row, jnp.zeros((5, BLK), jnp.int32)], axis=0
    )


def spread(values, axis, count):
    copies = jnp.broadcast_to(values[None], (count,) + values.shape)
    return lax.all_to_all(copies, axis, 0, 0)


def local(
    item_first, item_second, lengths, block_mask, core_first, core_second, w_proj, w_out, cotangent
):
    me = lax.axis_index("ctx").astype(jnp.int32)
    weights = lax.all_gather(pack_weights(w_proj, w_out), "dp", axis=0, tiled=True)
    weights = weights.reshape(NDP, 80, D)
    table = spread(jnp.concatenate([core_first, core_second], axis=0), "dp", NDP)
    table = table.reshape(2 * ROWS, D)
    own_indices = pack_indices(item_first, item_second, block_mask)
    indices = spread(own_indices, "ctx", NBLK)
    mask = indices[:, 2, :NBLK]
    info = jnp.stack([me, lengths[0, 0], lengths[0, 1], me])
    inverse = 1.0 / lengths[0].astype(F32)
    upstream = cotangent[0]

    normed_t, own_terms, own_embedded = embed_stage(info, indices, table)
    layer_out, grads, gate_grads, keys_head, values_head, queries_head, slopes = forward_stage(
        info, inverse, mask, normed_t, own_embedded, weights, upstream
    )
    grads = lax.all_to_all(grads, "ctx", 0, 0).reshape(SEQ, HD)
    pre_grads = backward_stage(
        info, inverse, mask, keys_head, values_head, queries_head, grads, slopes
    )
    groups = [[4 * c + h for h in range(4)] for c in range(4)]
    head_grads = lax.all_to_all(pre_grads, "ctx", 0, 0, axis_index_groups=groups)
    partial = core_stage(
        gate_grads, head_grads, weights, upstream, own_embedded, own_terms, own_indices
    )
    received = lax.all_to_all(partial.reshape(NDP, 8, D), "dp", 0, 0)
    pair_sum = jnp.sum(received.astype(F32), axis=0).astype(BF16)
    total = jnp.sum(spread(pair_sum, "ctx", NBLK).astype(F32), axis=0)
    return (layer_out[None], total[:4], total[4:])


def solution(mesh):
    placed = (
        P("dp", "ctx"),
        P("dp", "ctx"),
        P("dp", None),
        P("dp", "ctx", None),
        P("dp", None),
        P("dp", None),
        P(None, "dp"),
        P(None, "dp"),
        P("dp", "ctx", None),
    )
    return jax.shard_map(
        local,
        mesh=mesh,
        in_specs=placed,
        out_specs=(P("dp", "ctx", None), P("dp", None), P("dp", None)),
        check_vma=False,
    )
```

```python
import jax
import jax.numpy as jnp
from jax import lax
from jax.experimental import pallas as pl
from jax.experimental.pallas import tpu as pltpu
from jax.sharding import PartitionSpec as P

DA = 32
DB = 32
D = 1024
R = 32
ROWS = 128
H = 4
HD = 128
E = 512
BLK = 128
SEQ = 2048
NBLK = 16
TILE = 256
NDP = 32
CHUNK = 512
WIDE = 8
FORWARD_MB = 56
PREPARE_MB = 60
CORES_MB = 20

EPSILON = 1e-05
SCALE = HD ** (-0.5)
F32 = jnp.float32
BF16 = jnp.bfloat16
NT_DIMS = (((1,), (1,)), ((), ()))

SMEM_SPEC = pl.BlockSpec(memory_space=pltpu.SMEM)
VMEM_SPEC = pl.BlockSpec(memory_space=pltpu.VMEM)
HBM_SPEC = pl.BlockSpec(memory_space=pltpu.HBM)


def mm(left, right):
    return jnp.dot(left, right, preferred_element_type=F32)


def mm_nt(left, right):
    return lax.dot_general(left, right, NT_DIMS, preferred_element_type=F32)


def sigmoid(values):
    return 0.5 * jnp.tanh(0.5 * values) + 0.5


def silu(values):
    return values * sigmoid(values)


def silu_slope(values):
    sig = sigmoid(values)
    return sig * (1.0 + values * (1.0 - sig))


def flip(values):
    return values.astype(F32).T


def normalize(values, axis):
    average = jnp.mean(values, axis=axis, keepdims=True)
    centred = values - average
    inv_scale = lax.rsqrt(jnp.mean(centred * centred, axis=axis, keepdims=True) + EPSILON)
    return (centred * inv_scale, inv_scale)


def norm_back(upstream, normed, inv_scale):
    return (
        upstream
        - jnp.mean(upstream, axis=-1, keepdims=True)
        - normed * jnp.mean(upstream * normed, axis=-1, keepdims=True)
    ) * inv_scale


def pair_onehot(firsts, seconds):
    row = lax.broadcasted_iota(jnp.int32, (2 * ROWS, BLK), 0)
    core_row = ((row >> 3) << 2) | (row & 3)
    of_first = (row & 4) == 0
    hot_first = jnp.where(of_first & (core_row == firsts), 1.0, 0.0)
    hot_second = jnp.where((~of_first) & (core_row == seconds), 1.0, 0.0)
    return jnp.concatenate([hot_first, hot_second], axis=1).astype(BF16)


def aligned(index, unit):
    return pl.multiple_of(index * unit, unit)


def user_end(last_pos, first_len):
    return jnp.where(last_pos < first_len, first_len, SEQ)


def user_start(first_pos, first_len):
    return jnp.where(first_pos < first_len, 0, first_len)


def up_tiles(pos):
    return (pos + (TILE - 1)) // TILE


def block_range(chunk, first_len):
    low = (user_start(chunk * CHUNK, first_len) // TILE) * 2
    high = up_tiles(user_end(chunk * CHUNK + CHUNK - 1, first_len)) * 2
    return low, jnp.maximum(low, high - 12), high


def turn_table(table, table_t):
    for part in range(8):
        table_t[part * 128 : (part + 1) * 128, :] = flip(
            table[:, part * 128 : (part + 1) * 128]
        ).astype(BF16)


def embed_block(indices, position, table_t, rows_first, rows_second, emb):
    hot = pair_onehot(indices[position, 0:1, :], indices[position, 1:2, :])
    picked = mm(table_t[...], hot)
    rows_first[...] = picked[:, :BLK]
    rows_second[...] = picked[:, BLK:]

    def group(step, inner):
        base = aligned(step, WIDE * 32)
        sums = [jnp.zeros((DB, BLK), F32) for _ in range(WIDE)]
        for r in range(R):
            second = rows_second[r * DB : (r + 1) * DB, :]
            for k in range(WIDE):
                first = rows_first[pl.ds(base + (k * R + r), 1), :]
                sums[k] = sums[k] + first * second
        for k in range(WIDE):
            emb[pl.ds(pl.multiple_of(base + k * DB, DB), DB), :] = sums[k]
        return inner

    lax.fori_loop(0, DA // WIDE, group, 0)
    rounded = emb[...].astype(BF16)
    normed, unused = normalize(rounded.astype(F32), 0)
    return rounded, normed.astype(BF16)


def embed_kernel(
    info,
    indices,
    table,
    normed_far,
    own_terms,
    own_embedded,
    table_t,
    rows_first,
    rows_second,
    emb,
    normed_t,
    semaphores,
):
    me = info[0]
    unused, middle, high = block_range(me // 4, info[1])
    turn_table(table, table_t)

    def send(position):
        columns = pl.ds(aligned(position, BLK), BLK)
        return pltpu.make_async_copy(
            normed_t.at[:, columns], normed_far.at[:, columns], semaphores.at[position]
        )

    def block(position, carry):
        rounded, normed = embed_block(indices, position, table_t, rows_first, rows_second, emb)
        normed_t[:, pl.ds(aligned(position, BLK), BLK)] = normed
        send(position).start()

        @pl.when(position == me)
        def _():
            own_terms[0] = rows_first[...]
            own_terms[1] = rows_second[...]
            own_embedded[...] = rounded

        return carry

    def finish(position, carry):
        send(position).wait()
        return carry

    lax.fori_loop(middle, high, block, 0)
    lax.fori_loop(middle, high, finish, 0)


def weight_rows(weights, block, first=0, count=8):
    return weights[block * 8 + first : block * 8 + first + count, 0:64, :].reshape(count * 64, D)


def tile_scaling(row_first, column_first, shape, row_is_query, first_len, inverse, keep_low, keep_high):
    rows = row_first + lax.broadcasted_iota(jnp.int32, shape, 0)
    columns = column_first + lax.broadcasted_iota(jnp.int32, shape, 1)
    half = lax.broadcasted_iota(jnp.int32, shape, 1) < BLK
    query, key = (rows, columns) if row_is_query else (columns, rows)
    query_user = (query >= first_len).astype(jnp.int32)
    key_user = (key >= first_len).astype(jnp.int32)
    allowed = jnp.where(half, keep_low, keep_high)
    keep = (key >= query) & (query_user == key_user) & (allowed == 1)
    return jnp.where(keep, jnp.where(query_user == 1, inverse[1], inverse[0]), 0.0)


def fetch(source, target, semaphore):
    copy = pltpu.make_async_copy(source, target, semaphore)
    copy.start()
    return copy


def fetch_weights(far, near, semaphores, order):
    parts = [pl.ds(block * 8, 8) for block in order]
    return [
        fetch(far.at[part], near.at[part], semaphores.at[place])
        for place, part in enumerate(parts)
    ]


def tile_copy(far, near, semaphores, position):
    columns = pl.ds(aligned(position, TILE), TILE)
    return pltpu.make_async_copy(far.at[:, columns], near.at[:, columns], semaphores.at[position])


def forward_kernel(
    info,
    inverse,
    mask,
    normed_far,
    weights_far,
    cotangent,
    grads_out,
    gate_out,
    hidden_out,
    keys_head,
    values_head,
    out_t,
    keys_t,
    values_t,
    mixed,
    queries,
    weights,
    normed_t,
    semaphores,
    tile_semaphores,
):
    copies = fetch_weights(weights_far, weights, semaphores, (1, 3, 2, 0))
    me = info[0]
    first_len = info[1]
    chunk = me // 4
    head = me % 4
    kv_low = chunk * 2
    kv_high = up_tiles(user_end(chunk * CHUNK + CHUNK - 1, first_len))

    def begin(position, carry):
        tile_copy(normed_far, normed_t, tile_semaphores, position).start()
        return carry

    lax.fori_loop(kv_low, kv_high, begin, 0)
    copies[0].wait()
    copies[1].wait()

    def kv_tile(position, carry):
        columns = pl.ds(aligned(position, TILE), TILE)
        tile_copy(normed_far, normed_t, tile_semaphores, position).wait()
        piece = normed_t[:, columns]
        values_t[:, columns] = silu(mm(weight_rows(weights, 1), piece)).astype(BF16)
        keys_t[:, columns] = silu(mm(weight_rows(weights, 3), piece)).astype(BF16)
        return carry

    lax.fori_loop(kv_low, kv_high, kv_tile, 0)
    head_rows = pl.ds(aligned(head, HD), HD)
    keys_head[...] = keys_t[head_rows, :]
    values_head[...] = values_t[head_rows, :]
    copies[2].wait()
    copies[3].wait()

    for owner in range(NDP):
        out_t[owner * 32 : owner * 32 + 16, :] = weights[owner, 64:80, :E]
        out_t[owner * 32 + 16 : owner * 32 + 32, :] = weights[owner, 64:80, E:]

    own_normed = flip(normed_t[:, pl.ds(aligned(me, BLK), BLK)]).astype(BF16)
    pre_gate = mm_nt(own_normed, weight_rows(weights, 0))
    gate = silu(pre_gate).astype(BF16).astype(F32)
    queries[...] = silu(mm_nt(own_normed, weight_rows(weights, 2))).astype(BF16)
    mixed[...] = jnp.zeros((BLK, E), F32)

    def attend(position, carry):
        columns = pl.ds(aligned(position, TILE), TILE)
        scaling = tile_scaling(
            me * BLK,
            position * TILE,
            (BLK, TILE),
            True,
            first_len,
            inverse,
            mask[me, position * 2],
            mask[me, position * 2 + 1],
        )
        for h in range(H):
            own = slice(h * HD, (h + 1) * HD)
            scores = mm(queries[:, own], keys_t[own, columns]) * SCALE
            attention = (silu(scores) * scaling).astype(BF16)
            mixed[:, own] += mm_nt(attention, values_t[own, columns])
        return carry

    lax.fori_loop(me // 2, up_tiles(user_end(me * BLK + BLK - 1, first_len)), attend, 0)

    hidden_grad = mm(cotangent[...], out_t[...])
    mixed_normed, mixed_scale = normalize(mixed[...], -1)
    mixed_grad = norm_back(hidden_grad * gate, mixed_normed, mixed_scale).astype(BF16)
    for place in range(NBLK):
        h = place % 4
        grads_out[place] = mixed_grad[:, h * HD : (h + 1) * HD]
    hidden_out[...] = (mixed_normed * gate).astype(BF16)
    gate_out[...] = (hidden_grad * mixed_normed * silu_slope(pre_gate)).astype(BF16)


def prepare_kernel(
    info,
    indices,
    table,
    normed_far,
    own_embedded,
    weights_far,
    hidden,
    out_t,
    layer_out,
    queries_head,
    slopes_out,
    table_t,
    rows_first,
    rows_second,
    emb,
    normed_t,
    head_weights,
    semaphores,
    tile_semaphores,
):
    me = info[0]
    first_len = info[1]
    chunk = me // 4
    head = me % 4
    copies = [
        fetch(
            weights_far.at[pl.ds(block * 8 + head * 2, 2)],
            head_weights.at[block - 1],
            semaphores.at[block - 1],
        )
        for block in (1, 2, 3)
    ]
    low, middle, unused = block_range(chunk, first_len)
    q_low = low // 2
    q_middle = jnp.minimum(middle, chunk * 4) // 2
    q_high = chunk * 2 + 2

    def begin(position, carry):
        tile_copy(normed_far, normed_t, tile_semaphores, position).start()
        return carry

    def finish(position, carry):
        tile_copy(normed_far, normed_t, tile_semaphores, position).wait()
        return carry

    lax.fori_loop(q_middle, q_high, begin, 0)
    turn_table(table, table_t)

    def late_block(position, carry):
        unused, normed = embed_block(indices, position, table_t, rows_first, rows_second, emb)
        normed_t[:, pl.ds(aligned(position, BLK), BLK)] = normed
        return carry

    lax.fori_loop(low, q_middle * 2, late_block, 0)
    layer_out[...] = (flip(own_embedded[...]) + mm_nt(hidden[...], out_t[...])).astype(BF16)
    for copy in copies:
        copy.wait()
    lax.fori_loop(q_middle, q_high, finish, 0)

    def rows_of(place):
        return head_weights[place, :, 0:64, :].reshape(HD, D)

    def q_tile(position, carry):
        tile = pl.ds(aligned(position, TILE), TILE)
        queries_head[:, tile] = silu(mm(rows_of(1), normed_t[:, tile])).astype(BF16)
        return carry

    lax.fori_loop(q_low, q_high, q_tile, 0)
    chunk_piece = normed_t[:, pl.ds(aligned(chunk, CHUNK), CHUNK)]
    for place in range(3):
        slopes_out[:, place * HD : (place + 1) * HD] = silu_slope(
            mm(rows_of(place), chunk_piece)
        ).T


def backward_kernel(
    info,
    inverse,
    mask,
    keys_head,
    values_head,
    queries_head,
    grads,
    slopes,
    weights_far,
    pre_grads,
    weights,
    own_keys,
    own_values,
    own_queries,
    sums,
    semaphores,
):
    copies = fetch_weights(weights_far, weights, semaphores, (0, 1, 2, 3))
    me = info[0]
    first_len = info[1]
    chunk = me // 4
    columns = pl.ds(aligned(chunk, CHUNK), CHUNK)
    own_keys[...] = flip(keys_head[:, columns]).astype(BF16)
    own_values[...] = flip(values_head[:, columns]).astype(BF16)
    own_queries[...] = flip(queries_head[:, columns]).astype(BF16)
    for part in range(4):
        block = chunk * 4 + part
        rows = slice(part * BLK, (part + 1) * BLK)
        sums[...] = jnp.zeros((BLK, 3 * HD), F32)

        def query_side(position, carry):
            tile = pl.ds(aligned(position, TILE), TILE)
            scaling = tile_scaling(
                block * BLK,
                position * TILE,
                (BLK, TILE),
                True,
                first_len,
                inverse,
                mask[block, position * 2],
                mask[block, position * 2 + 1],
            )
            scores = mm(own_queries[rows, :], keys_head[:, tile]) * SCALE
            pressure = mm(grads[pl.ds(aligned(block, BLK), BLK), :], values_head[:, tile])
            score_grad = (pressure * silu_slope(scores) * scaling).astype(BF16)
            sums[:, HD : 2 * HD] += mm_nt(score_grad, keys_head[:, tile])
            return carry

        lax.fori_loop(
            block // 2, up_tiles(user_end(block * BLK + BLK - 1, first_len)), query_side, 0
        )

        def key_side(position, carry):
            tile = pl.ds(aligned(position, TILE), TILE)
            scaling = tile_scaling(
                block * BLK,
                position * TILE,
                (BLK, TILE),
                False,
                first_len,
                inverse,
                mask[position * 2, block],
                mask[position * 2 + 1, block],
            )
            scores = mm(own_keys[rows, :], queries_head[:, tile]) * SCALE
            sig = sigmoid(scores)
            grad_tile = grads[tile, :]
            attention = (scores * sig * scaling).astype(BF16)
            pressure = mm_nt(own_values[rows, :], grad_tile)
            slope = sig * (1.0 + scores * (1.0 - sig))
            score_grad = (pressure * slope * scaling).astype(BF16)
            sums[:, :HD] += mm(attention, grad_tile)
            sums[:, 2 * HD :] += mm_nt(score_grad, queries_head[:, tile])
            return carry

        lax.fori_loop(
            user_start(block * BLK, first_len) // TILE, block // 2 + 1, key_side, 0
        )
        pre_grads[part, :, :HD] = (sums[:, :HD] * slopes[rows, :HD]).astype(BF16)
        pre_grads[part, :, HD:] = (sums[:, HD:] * SCALE * slopes[rows, HD:]).astype(BF16)
    for copy in copies:
        copy.wait()


def core_kernel(
    gate_grads,
    head_grads,
    weights,
    cotangent,
    own_embedded,
    own_terms,
    indices,
    partial_out,
    rows_second,
    grad_t,
    terms,
):
    x_normed, x_scale = normalize(flip(own_embedded[...]), -1)
    normed_grad = mm(gate_grads[...], weight_rows(weights, 0))
    for place in range(3):
        joined = jnp.concatenate(
            [head_grads[h, :, place * HD : (place + 1) * HD] for h in range(H)], axis=1
        )
        normed_grad = normed_grad + mm(joined, weight_rows(weights, place + 1))
    input_grad = cotangent[...].astype(F32) + norm_back(normed_grad, x_normed, x_scale)
    grad_t[...] = input_grad.T
    for b in range(DB):
        rows_second[b * R : (b + 1) * R, :] = own_terms.at[1][pl.ds(b, R, stride=DB), :]

    def group(step, carry):
        base = aligned(step, WIDE * 32)
        sums = [jnp.zeros((R, BLK), F32) for _ in range(WIDE)]
        for b in range(DB):
            second = rows_second[b * R : (b + 1) * R, :]
            for k in range(WIDE):
                sums[k] = sums[k] + grad_t[pl.ds(base + (k * DB + b), 1), :] * second
        for k in range(WIDE):
            terms[pl.ds(pl.multiple_of(base + k * R, R), R), :BLK] = sums[k]
        sums = [jnp.zeros((DB, BLK), F32) for _ in range(WIDE)]
        for a in range(DA):
            grad = grad_t[a * DB : (a + 1) * DB, :]
            for k in range(WIDE):
                first = own_terms[0, pl.ds(a * R + step * WIDE + k, 1), :]
                sums[k] = sums[k] + first * grad
        for k in range(WIDE):
            terms[pl.ds(pl.multiple_of(base + k * DB, DB), DB), BLK:] = sums[k]
        return carry

    lax.fori_loop(0, DA // WIDE, group, 0)
    hot = pair_onehot(indices[0:1, :], indices[1:2, :])
    whole = terms[...]
    upper = whole.astype(BF16)
    lower = (whole - upper.astype(F32)).astype(BF16)
    total = mm_nt(hot, upper) + mm_nt(hot, lower)
    partial_out[...] = total.astype(BF16)


def params(megabytes):
    return pltpu.CompilerParams(vmem_limit_bytes=megabytes * 1024 * 1024)


def shape(dims, kind):
    return jax.ShapeDtypeStruct(dims, kind)


def embed_stage(info, indices, table):
    return pl.pallas_call(
        embed_kernel,
        out_shape=(shape((D, SEQ), BF16), shape((2, D, BLK), F32), shape((D, BLK), BF16)),
        in_specs=[SMEM_SPEC, VMEM_SPEC, VMEM_SPEC],
        out_specs=(HBM_SPEC, VMEM_SPEC, VMEM_SPEC),
        scratch_shapes=[
            pltpu.VMEM((D, 2 * ROWS), BF16),
            pltpu.VMEM((D, BLK), F32),
            pltpu.VMEM((D, BLK), F32),
            pltpu.VMEM((D, BLK), F32),
            pltpu.VMEM((D, SEQ), BF16),
            pltpu.SemaphoreType.DMA((NBLK,)),
        ],
        compiler_params=params(57),
        cost_estimate=pl.CostEstimate(flops=20_000_000_000, bytes_accessed=6_000_000, transcendentals=0),
        name="embed",
    )(info, indices, table)


def cost(flops, moved):
    return pl.CostEstimate(flops=flops, bytes_accessed=moved, transcendentals=0)


def forward_stage(info, inverse, mask, normed_t, weights, cotangent):
    return pl.pallas_call(
        forward_kernel,
        out_shape=(
            shape((NBLK, BLK, HD), BF16),
            shape((BLK, E), BF16),
            shape((BLK, E), BF16),
            shape((HD, SEQ), BF16),
            shape((HD, SEQ), BF16),
            shape((D, E), BF16),
        ),
        in_specs=[SMEM_SPEC] * 3 + [HBM_SPEC, HBM_SPEC, VMEM_SPEC],
        out_specs=(VMEM_SPEC,) * 6,
        scratch_shapes=[
            pltpu.VMEM((E, SEQ), BF16),
            pltpu.VMEM((E, SEQ), BF16),
            pltpu.VMEM((BLK, E), F32),
            pltpu.VMEM((BLK, E), BF16),
            pltpu.VMEM((NDP, 80, D), BF16),
            pltpu.VMEM((D, SEQ), BF16),
            pltpu.SemaphoreType.DMA((4,)),
            pltpu.SemaphoreType.DMA((8,)),
        ],
        compiler_params=params(FORWARD_MB),
        cost_estimate=cost(8_000_000_000, 12_000_000),
        name="forward",
    )(info, inverse, mask, normed_t, weights, cotangent)


def prepare_stage(info, indices, table, normed_t, own_embedded, weights, hidden, out_t):
    return pl.pallas_call(
        prepare_kernel,
        out_shape=(
            shape((BLK, D), BF16),
            shape((HD, SEQ), BF16),
            shape((CHUNK, 3 * HD), F32),
        ),
        in_specs=[
            SMEM_SPEC,
            VMEM_SPEC,
            VMEM_SPEC,
            HBM_SPEC,
            VMEM_SPEC,
            HBM_SPEC,
            VMEM_SPEC,
            VMEM_SPEC,
        ],
        out_specs=(VMEM_SPEC,) * 3,
        scratch_shapes=[
            pltpu.VMEM((D, 2 * ROWS), BF16),
            pltpu.VMEM((D, BLK), F32),
            pltpu.VMEM((D, BLK), F32),
            pltpu.VMEM((D, BLK), F32),
            pltpu.VMEM((D, SEQ), BF16),
            pltpu.VMEM((3, 2, 80, D), BF16),
            pltpu.SemaphoreType.DMA((3,)),
            pltpu.SemaphoreType.DMA((8,)),
        ],
        compiler_params=params(PREPARE_MB),
        cost_estimate=cost(5_000_000_000, 6_000_000),
        name="prepare",
    )(info, indices, table, normed_t, own_embedded, weights, hidden, out_t)


def backward_stage(
    info, inverse, mask, keys_head, values_head, queries_head, grads, slopes, weights
):
    return pl.pallas_call(
        backward_kernel,
        out_shape=(shape((4, BLK, 3 * HD), BF16), shape((NDP, 80, D), BF16)),
        in_specs=[SMEM_SPEC] * 3 + [VMEM_SPEC] * 5 + [HBM_SPEC],
        out_specs=(VMEM_SPEC, VMEM_SPEC),
        scratch_shapes=[pltpu.VMEM((CHUNK, HD), BF16)] * 3
        + [pltpu.VMEM((BLK, 3 * HD), F32), pltpu.SemaphoreType.DMA((4,))],
        compiler_params=params(43),
        name="backward",
    )(info, inverse, mask, keys_head, values_head, queries_head, grads, slopes, weights)


def core_stage(gate_grads, head_grads, weights, cotangent, own_embedded, own_terms, indices):
    return pl.pallas_call(
        core_kernel,
        out_shape=shape((2 * ROWS, D), BF16),
        in_specs=[VMEM_SPEC] * 7,
        out_specs=VMEM_SPEC,
        scratch_shapes=[
            pltpu.VMEM((D, BLK), F32),
            pltpu.VMEM((D, BLK), F32),
            pltpu.VMEM((D, 2 * BLK), F32),
        ],
        compiler_params=params(CORES_MB),
        name="cores",
    )(gate_grads, head_grads, weights, cotangent, own_embedded, own_terms, indices)


def pack_weights(w_proj, w_out):
    out_t = w_out.T
    return jnp.concatenate([w_proj.T, jnp.concatenate([out_t[:16], out_t[16:]], axis=1)], axis=0)


def pack_indices(item_first, item_second, block_mask):
    mask_row = jnp.pad(block_mask[0], ((0, 0), (0, BLK - NBLK)))
    return jnp.concatenate(
        [item_first, item_second, mask_row, jnp.zeros((5, BLK), jnp.int32)], axis=0
    )


def spread(values, axis, count):
    copies = jnp.broadcast_to(values[None], (count,) + values.shape)
    return lax.all_to_all(copies, axis, 0, 0)


def local(
    item_first, item_second, lengths, block_mask, core_first, core_second, w_proj, w_out, cotangent
):
    me = lax.axis_index("ctx").astype(jnp.int32)
    weights = lax.all_gather(pack_weights(w_proj, w_out), "dp", axis=0, tiled=True)
    weights = weights.reshape(NDP, 80, D)
    table = spread(jnp.concatenate([core_first, core_second], axis=0), "dp", NDP)
    table = table.reshape(2 * ROWS, D)
    own_indices = pack_indices(item_first, item_second, block_mask)
    indices = spread(own_indices, "ctx", NBLK)
    mask = indices[:, 2, :NBLK]
    info = jnp.stack([me, lengths[0, 0], lengths[0, 1], me])
    inverse = 1.0 / lengths[0].astype(F32)
    upstream = cotangent[0]

    normed_t, own_terms, own_embedded = embed_stage(info, indices, table)
    grads, gate_grads, hidden, keys_head, values_head, out_t = forward_stage(
        info, inverse, mask, normed_t, weights, upstream
    )
    grads = lax.all_to_all(grads, "ctx", 0, 0).reshape(SEQ, HD)
    layer_out, queries_head, slopes = prepare_stage(
        info, indices, table, normed_t, own_embedded, weights, hidden, out_t
    )
    pre_grads, weights_near = backward_stage(
        info, inverse, mask, keys_head, values_head, queries_head, grads, slopes, weights
    )
    groups = [[4 * c + h for h in range(4)] for c in range(4)]
    head_grads = lax.all_to_all(pre_grads, "ctx", 0, 0, axis_index_groups=groups)
    partial = core_stage(
        gate_grads, head_grads, weights_near, upstream, own_embedded, own_terms, own_indices
    )
    received = lax.all_to_all(partial.reshape(NDP, 8, D), "dp", 0, 0)
    pair_sum = jnp.sum(received.astype(F32), axis=0).astype(BF16)
    total = jnp.sum(spread(pair_sum, "ctx", NBLK).astype(F32), axis=0)
    return (layer_out[None], total[:4], total[4:])


def solution(mesh):
    placed = (
        P("dp", "ctx"),
        P("dp", "ctx"),
        P("dp", None),
        P("dp", "ctx", None),
        P("dp", None),
        P("dp", None),
        P(None, "dp"),
        P(None, "dp"),
        P("dp", "ctx", None),
    )
    return jax.shard_map(
        local,
        mesh=mesh,
        in_specs=placed,
        out_specs=(P("dp", "ctx", None), P("dp", None), P("dp", None)),
        check_vma=False,
    )
```

```python
import jax
import jax.numpy as jnp
from jax import lax
from jax.experimental import pallas as pl
from jax.experimental.pallas import tpu as pltpu
from jax.sharding import PartitionSpec as P

DA = 32
DB = 32
D = 1024
R = 32
ROWS = 128
H = 4
HD = 128
E = 512
BLK = 128
SEQ = 2048
NBLK = 16
TILE = 256
NDP = 32
CHUNK = 512
WIDE = 8
FORWARD_MB = 56
PREPARE_MB = 50
CORES_MB = 20

EPSILON = 1e-05
SCALE = HD ** (-0.5)
F32 = jnp.float32
BF16 = jnp.bfloat16
NT_DIMS = (((1,), (1,)), ((), ()))

SMEM_SPEC = pl.BlockSpec(memory_space=pltpu.SMEM)
VMEM_SPEC = pl.BlockSpec(memory_space=pltpu.VMEM)
HBM_SPEC = pl.BlockSpec(memory_space=pltpu.HBM)


def mm(left, right):
    return jnp.dot(left, right, preferred_element_type=F32)


def mm_nt(left, right):
    return lax.dot_general(left, right, NT_DIMS, preferred_element_type=F32)


def sigmoid(values):
    return 0.5 * jnp.tanh(0.5 * values) + 0.5


def silu(values):
    return values * sigmoid(values)


def silu_slope(values):
    sig = sigmoid(values)
    return sig * (1.0 + values * (1.0 - sig))


def flip(values):
    return values.astype(F32).T


def normalize(values, axis):
    average = jnp.mean(values, axis=axis, keepdims=True)
    centred = values - average
    inv_scale = lax.rsqrt(jnp.mean(centred * centred, axis=axis, keepdims=True) + EPSILON)
    return (centred * inv_scale, inv_scale)


def norm_back(upstream, normed, inv_scale):
    return (
        upstream
        - jnp.mean(upstream, axis=-1, keepdims=True)
        - normed * jnp.mean(upstream * normed, axis=-1, keepdims=True)
    ) * inv_scale


def pair_onehot(firsts, seconds):
    row = lax.broadcasted_iota(jnp.int32, (2 * ROWS, BLK), 0)
    core_row = ((row >> 3) << 2) | (row & 3)
    of_first = (row & 4) == 0
    hot_first = jnp.where(of_first & (core_row == firsts), 1.0, 0.0)
    hot_second = jnp.where((~of_first) & (core_row == seconds), 1.0, 0.0)
    return jnp.concatenate([hot_first, hot_second], axis=1).astype(BF16)


def aligned(index, unit):
    return pl.multiple_of(index * unit, unit)


def user_end(last_pos, first_len):
    return jnp.where(last_pos < first_len, first_len, SEQ)


def user_start(first_pos, first_len):
    return jnp.where(first_pos < first_len, 0, first_len)


def up_tiles(pos):
    return (pos + (TILE - 1)) // TILE


def block_range(chunk, first_len):
    low = (user_start(chunk * CHUNK, first_len) // TILE) * 2
    high = up_tiles(user_end(chunk * CHUNK + CHUNK - 1, first_len)) * 2
    return low, jnp.maximum(low, high - 12), high


def turn_table(table, table_t):
    for part in range(8):
        table_t[part * 128 : (part + 1) * 128, :] = flip(
            table[:, part * 128 : (part + 1) * 128]
        ).astype(BF16)


def embed_block(indices, position, table_t, rows_first, rows_second, emb):
    hot = pair_onehot(indices[position, 0:1, :], indices[position, 1:2, :])
    picked = mm(table_t[...], hot)
    rows_first[...] = picked[:, :BLK]
    rows_second[...] = picked[:, BLK:]

    def group(step, inner):
        base = aligned(step, WIDE * 32)
        sums = [jnp.zeros((DB, BLK), F32) for _ in range(WIDE)]
        for r in range(R):
            second = rows_second[r * DB : (r + 1) * DB, :]
            for k in range(WIDE):
                first = rows_first[pl.ds(base + (k * R + r), 1), :]
                sums[k] = sums[k] + first * second
        for k in range(WIDE):
            emb[pl.ds(pl.multiple_of(base + k * DB, DB), DB), :] = sums[k]
        return inner

    lax.fori_loop(0, DA // WIDE, group, 0)
    rounded = emb[...].astype(BF16)
    normed, unused = normalize(rounded.astype(F32), 0)
    return rounded, normed.astype(BF16)


def embed_kernel(
    info,
    indices,
    table,
    normed_far,
    own_terms,
    own_embedded,
    table_t,
    rows_first,
    rows_second,
    emb,
    normed_t,
    semaphores,
):
    me = info[0]
    unused, middle, high = block_range(me // 4, info[1])
    turn_table(table, table_t)

    def send(position):
        columns = pl.ds(aligned(position, BLK), BLK)
        return pltpu.make_async_copy(
            normed_t.at[:, columns], normed_far.at[:, columns], semaphores.at[position]
        )

    def block(position, carry):
        rounded, normed = embed_block(indices, position, table_t, rows_first, rows_second, emb)
        normed_t[:, pl.ds(aligned(position, BLK), BLK)] = normed
        send(position).start()

        @pl.when(position == me)
        def _():
            own_terms[0] = rows_first[...]
            own_terms[1] = rows_second[...]
            own_embedded[...] = rounded

        return carry

    def finish(position, carry):
        send(position).wait()
        return carry

    lax.fori_loop(middle, high, block, 0)
    lax.fori_loop(middle, high, finish, 0)


def weight_rows(weights, block, first=0, count=8):
    return weights[block * 8 + first : block * 8 + first + count, 0:64, :].reshape(count * 64, D)


def tile_scaling(row_first, column_first, shape, row_is_query, first_len, inverse, keep_low, keep_high):
    rows = row_first + lax.broadcasted_iota(jnp.int32, shape, 0)
    columns = column_first + lax.broadcasted_iota(jnp.int32, shape, 1)
    half = lax.broadcasted_iota(jnp.int32, shape, 1) < BLK
    query, key = (rows, columns) if row_is_query else (columns, rows)
    query_user = (query >= first_len).astype(jnp.int32)
    key_user = (key >= first_len).astype(jnp.int32)
    allowed = jnp.where(half, keep_low, keep_high)
    keep = (key >= query) & (query_user == key_user) & (allowed == 1)
    return jnp.where(keep, jnp.where(query_user == 1, inverse[1], inverse[0]), 0.0)


def square_scaling(mask, row_tile, column_tile, first_len, inverse, row_is_query):
    dims = (TILE, TILE)
    rows = row_tile * TILE + lax.broadcasted_iota(jnp.int32, dims, 0)
    columns = column_tile * TILE + lax.broadcasted_iota(jnp.int32, dims, 1)
    row_half = lax.broadcasted_iota(jnp.int32, dims, 0) < BLK
    column_half = lax.broadcasted_iota(jnp.int32, dims, 1) < BLK

    def flag(row, column):
        row, column = row_tile * 2 + row, column_tile * 2 + column
        return mask[row, column] if row_is_query else mask[column, row]

    allowed = jnp.where(
        row_half,
        jnp.where(column_half, flag(0, 0), flag(0, 1)),
        jnp.where(column_half, flag(1, 0), flag(1, 1)),
    )
    query, key = (rows, columns) if row_is_query else (columns, rows)
    query_user = (query >= first_len).astype(jnp.int32)
    key_user = (key >= first_len).astype(jnp.int32)
    keep = (key >= query) & (query_user == key_user) & (allowed == 1)
    return jnp.where(keep, jnp.where(query_user == 1, inverse[1], inverse[0]), 0.0)


def fetch(source, target, semaphore):
    copy = pltpu.make_async_copy(source, target, semaphore)
    copy.start()
    return copy


def fetch_weights(far, near, semaphores, order):
    parts = [pl.ds(block * 8, 8) for block in order]
    return [
        fetch(far.at[part], near.at[part], semaphores.at[place])
        for place, part in enumerate(parts)
    ]


def tile_copy(far, near, semaphores, position):
    columns = pl.ds(aligned(position, TILE), TILE)
    return pltpu.make_async_copy(far.at[:, columns], near.at[:, columns], semaphores.at[position])


def forward_kernel(
    info,
    inverse,
    mask,
    normed_far,
    weights_far,
    cotangent,
    grads_out,
    gate_out,
    hidden_out,
    keys_head,
    values_head,
    out_t,
    keys_t,
    values_t,
    mixed,
    queries,
    weights,
    normed_t,
    semaphores,
    tile_semaphores,
):
    copies = fetch_weights(weights_far, weights, semaphores, (1, 3, 2, 0))
    me = info[0]
    first_len = info[1]
    chunk = me // 4
    head = me % 4
    kv_low = chunk * 2
    kv_high = up_tiles(user_end(chunk * CHUNK + CHUNK - 1, first_len))

    def begin(position, carry):
        tile_copy(normed_far, normed_t, tile_semaphores, position).start()
        return carry

    lax.fori_loop(kv_low, kv_high, begin, 0)
    copies[0].wait()
    copies[1].wait()

    def kv_tile(position, carry):
        columns = pl.ds(aligned(position, TILE), TILE)
        tile_copy(normed_far, normed_t, tile_semaphores, position).wait()
        piece = normed_t[:, columns]
        values_t[:, columns] = silu(mm(weight_rows(weights, 1), piece)).astype(BF16)
        keys_t[:, columns] = silu(mm(weight_rows(weights, 3), piece)).astype(BF16)
        return carry

    lax.fori_loop(kv_low, kv_high, kv_tile, 0)
    head_rows = pl.ds(aligned(head, HD), HD)
    keys_head[...] = keys_t[head_rows, :]
    values_head[...] = values_t[head_rows, :]
    copies[2].wait()
    copies[3].wait()

    for owner in range(NDP):
        out_t[owner * 32 : owner * 32 + 16, :] = weights[owner, 64:80, :E]
        out_t[owner * 32 + 16 : owner * 32 + 32, :] = weights[owner, 64:80, E:]

    own_normed = flip(normed_t[:, pl.ds(aligned(me, BLK), BLK)]).astype(BF16)
    pre_gate = mm_nt(own_normed, weight_rows(weights, 0))
    gate = silu(pre_gate).astype(BF16).astype(F32)
    queries[...] = silu(mm_nt(own_normed, weight_rows(weights, 2))).astype(BF16)
    mixed[...] = jnp.zeros((BLK, E), F32)

    def attend(position, carry):
        columns = pl.ds(aligned(position, TILE), TILE)
        scaling = tile_scaling(
            me * BLK,
            position * TILE,
            (BLK, TILE),
            True,
            first_len,
            inverse,
            mask[me, position * 2],
            mask[me, position * 2 + 1],
        )
        for h in range(H):
            own = slice(h * HD, (h + 1) * HD)
            scores = mm(queries[:, own], keys_t[own, columns]) * SCALE
            attention = (silu(scores) * scaling).astype(BF16)
            mixed[:, own] += mm_nt(attention, values_t[own, columns])
        return carry

    lax.fori_loop(me // 2, up_tiles(user_end(me * BLK + BLK - 1, first_len)), attend, 0)

    hidden_grad = mm(cotangent[...], out_t[...])
    mixed_normed, mixed_scale = normalize(mixed[...], -1)
    mixed_grad = norm_back(hidden_grad * gate, mixed_normed, mixed_scale).astype(BF16)
    for place in range(NBLK):
        h = place % 4
        grads_out[place] = mixed_grad[:, h * HD : (h + 1) * HD]
    hidden_out[...] = (mixed_normed * gate).astype(BF16)
    gate_out[...] = (hidden_grad * mixed_normed * silu_slope(pre_gate)).astype(BF16)


def prepare_kernel(
    info,
    indices,
    table,
    normed_far,
    own_embedded,
    weights_far,
    hidden,
    out_t,
    layer_out,
    queries_head,
    slopes_out,
    table_t,
    rows_first,
    rows_second,
    emb,
    normed_t,
    head_weights,
    semaphores,
    tile_semaphores,
):
    me = info[0]
    first_len = info[1]
    chunk = me // 4
    head = me % 4
    copies = [
        fetch(
            weights_far.at[pl.ds(block * 8 + head * 2, 2)],
            head_weights.at[block - 1],
            semaphores.at[block - 1],
        )
        for block in (1, 2, 3)
    ]
    low, middle, unused = block_range(chunk, first_len)
    q_low = low // 2
    q_middle = jnp.minimum(middle, chunk * 4) // 2
    q_high = chunk * 2 + 2

    def begin(position, carry):
        tile_copy(normed_far, normed_t, tile_semaphores, position).start()
        return carry

    def finish(position, carry):
        tile_copy(normed_far, normed_t, tile_semaphores, position).wait()
        return carry

    lax.fori_loop(q_middle, q_high, begin, 0)
    turn_table(table, table_t)

    def late_block(position, carry):
        unused, normed = embed_block(indices, position, table_t, rows_first, rows_second, emb)
        normed_t[:, pl.ds(aligned(position, BLK), BLK)] = normed
        return carry

    lax.fori_loop(low, q_middle * 2, late_block, 0)
    layer_out[...] = (flip(own_embedded[...]) + mm_nt(hidden[...], out_t[...])).astype(BF16)
    for copy in copies:
        copy.wait()
    lax.fori_loop(q_middle, q_high, finish, 0)

    def rows_of(place):
        return head_weights[place, :, 0:64, :].reshape(HD, D)

    def q_tile(position, carry):
        tile = pl.ds(aligned(position, TILE), TILE)
        queries_head[:, tile] = silu(mm(rows_of(1), normed_t[:, tile])).astype(BF16)
        return carry

    lax.fori_loop(q_low, q_high, q_tile, 0)
    chunk_piece = normed_t[:, pl.ds(aligned(chunk, CHUNK), CHUNK)]
    for place in range(3):
        slopes_out[:, place * HD : (place + 1) * HD] = silu_slope(
            mm(rows_of(place), chunk_piece)
        ).T


def backward_kernel(
    info,
    inverse,
    mask,
    keys_head,
    values_head,
    queries_head,
    grads,
    slopes,
    weights_far,
    pre_grads,
    weights,
    own_keys,
    own_values,
    own_queries,
    sums,
    semaphores,
):
    copies = fetch_weights(weights_far, weights, semaphores, (0, 1, 2, 3))
    me = info[0]
    first_len = info[1]
    chunk = me // 4
    columns = pl.ds(aligned(chunk, CHUNK), CHUNK)
    own_keys[...] = flip(keys_head[:, columns]).astype(BF16)
    own_values[...] = flip(values_head[:, columns]).astype(BF16)
    own_queries[...] = flip(queries_head[:, columns]).astype(BF16)
    for part in range(2):
        place = chunk * 2 + part
        rows = slice(part * TILE, (part + 1) * TILE)
        sums[...] = jnp.zeros((TILE, 3 * HD), F32)

        def query_side(position, carry):
            tile = pl.ds(aligned(position, TILE), TILE)
            scaling = square_scaling(mask, place, position, first_len, inverse, True)
            scores = mm(own_queries[rows, :], keys_head[:, tile]) * SCALE
            pressure = mm(grads[pl.ds(aligned(place, TILE), TILE), :], values_head[:, tile])
            score_grad = (pressure * silu_slope(scores) * scaling).astype(BF16)
            sums[:, HD : 2 * HD] += mm_nt(score_grad, keys_head[:, tile])
            return carry

        lax.fori_loop(
            place, up_tiles(user_end(place * TILE + TILE - 1, first_len)), query_side, 0
        )

        def key_side(position, carry):
            tile = pl.ds(aligned(position, TILE), TILE)
            scaling = square_scaling(mask, place, position, first_len, inverse, False)
            scores = mm(own_keys[rows, :], queries_head[:, tile]) * SCALE
            sig = sigmoid(scores)
            grad_tile = grads[tile, :]
            attention = (scores * sig * scaling).astype(BF16)
            pressure = mm_nt(own_values[rows, :], grad_tile)
            slope = sig * (1.0 + scores * (1.0 - sig))
            score_grad = (pressure * slope * scaling).astype(BF16)
            sums[:, :HD] += mm(attention, grad_tile)
            sums[:, 2 * HD :] += mm_nt(score_grad, queries_head[:, tile])
            return carry

        lax.fori_loop(user_start(place * TILE, first_len) // TILE, place + 1, key_side, 0)
        for half in range(2):
            near = slice(half * BLK, (half + 1) * BLK)
            far = slice(part * TILE + half * BLK, part * TILE + (half + 1) * BLK)
            block = part * 2 + half
            pre_grads[block, :, :HD] = (sums[near, :HD] * slopes[far, :HD]).astype(BF16)
            pre_grads[block, :, HD:] = (sums[near, HD:] * SCALE * slopes[far, HD:]).astype(BF16)
    for copy in copies:
        copy.wait()


def core_kernel(
    gate_grads,
    head_grads,
    weights,
    cotangent,
    own_embedded,
    own_terms,
    indices,
    partial_out,
    rows_second,
    grad_t,
    terms,
):
    x_normed, x_scale = normalize(flip(own_embedded[...]), -1)
    normed_grad = mm(gate_grads[...], weight_rows(weights, 0))
    for place in range(3):
        joined = jnp.concatenate(
            [head_grads[h, :, place * HD : (place + 1) * HD] for h in range(H)], axis=1
        )
        normed_grad = normed_grad + mm(joined, weight_rows(weights, place + 1))
    input_grad = cotangent[...].astype(F32) + norm_back(normed_grad, x_normed, x_scale)
    grad_t[...] = input_grad.T
    for b in range(DB):
        rows_second[b * R : (b + 1) * R, :] = own_terms.at[1][pl.ds(b, R, stride=DB), :]

    def group(step, carry):
        base = aligned(step, WIDE * 32)
        sums = [jnp.zeros((R, BLK), F32) for _ in range(WIDE)]
        for b in range(DB):
            second = rows_second[b * R : (b + 1) * R, :]
            for k in range(WIDE):
                sums[k] = sums[k] + grad_t[pl.ds(base + (k * DB + b), 1), :] * second
        for k in range(WIDE):
            terms[pl.ds(pl.multiple_of(base + k * R, R), R), :BLK] = sums[k]
        sums = [jnp.zeros((DB, BLK), F32) for _ in range(WIDE)]
        for a in range(DA):
            grad = grad_t[a * DB : (a + 1) * DB, :]
            for k in range(WIDE):
                first = own_terms[0, pl.ds(a * R + step * WIDE + k, 1), :]
                sums[k] = sums[k] + first * grad
        for k in range(WIDE):
            terms[pl.ds(pl.multiple_of(base + k * DB, DB), DB), BLK:] = sums[k]
        return carry

    lax.fori_loop(0, DA // WIDE, group, 0)
    hot = pair_onehot(indices[0:1, :], indices[1:2, :])
    whole = terms[...]
    upper = whole.astype(BF16)
    lower = (whole - upper.astype(F32)).astype(BF16)
    total = mm_nt(hot, upper) + mm_nt(hot, lower)
    partial_out[...] = total.astype(BF16)


def params(megabytes):
    return pltpu.CompilerParams(vmem_limit_bytes=megabytes * 1024 * 1024)


def shape(dims, kind):
    return jax.ShapeDtypeStruct(dims, kind)


def embed_stage(info, indices, table):
    return pl.pallas_call(
        embed_kernel,
        out_shape=(shape((D, SEQ), BF16), shape((2, D, BLK), F32), shape((D, BLK), BF16)),
        in_specs=[SMEM_SPEC, VMEM_SPEC, VMEM_SPEC],
        out_specs=(HBM_SPEC, VMEM_SPEC, VMEM_SPEC),
        scratch_shapes=[
            pltpu.VMEM((D, 2 * ROWS), BF16),
            pltpu.VMEM((D, BLK), F32),
            pltpu.VMEM((D, BLK), F32),
            pltpu.VMEM((D, BLK), F32),
            pltpu.VMEM((D, SEQ), BF16),
            pltpu.SemaphoreType.DMA((NBLK,)),
        ],
        compiler_params=params(57),
        cost_estimate=pl.CostEstimate(flops=20_000_000_000, bytes_accessed=6_000_000, transcendentals=0),
        name="embed",
    )(info, indices, table)


def cost(flops, moved):
    return pl.CostEstimate(flops=flops, bytes_accessed=moved, transcendentals=0)


def forward_stage(info, inverse, mask, normed_t, weights, cotangent):
    return pl.pallas_call(
        forward_kernel,
        out_shape=(
            shape((NBLK, BLK, HD), BF16),
            shape((BLK, E), BF16),
            shape((BLK, E), BF16),
            shape((HD, SEQ), BF16),
            shape((HD, SEQ), BF16),
            shape((D, E), BF16),
        ),
        in_specs=[SMEM_SPEC] * 3 + [HBM_SPEC, HBM_SPEC, VMEM_SPEC],
        out_specs=(VMEM_SPEC,) * 6,
        scratch_shapes=[
            pltpu.VMEM((E, SEQ), BF16),
            pltpu.VMEM((E, SEQ), BF16),
            pltpu.VMEM((BLK, E), F32),
            pltpu.VMEM((BLK, E), BF16),
            pltpu.VMEM((NDP, 80, D), BF16),
            pltpu.VMEM((D, SEQ), BF16),
            pltpu.SemaphoreType.DMA((4,)),
            pltpu.SemaphoreType.DMA((8,)),
        ],
        compiler_params=params(FORWARD_MB),
        cost_estimate=cost(8_000_000_000, 12_000_000),
        name="forward",
    )(info, inverse, mask, normed_t, weights, cotangent)


def prepare_stage(info, indices, table, normed_t, own_embedded, weights, hidden, out_t):
    return pl.pallas_call(
        prepare_kernel,
        out_shape=(
            shape((BLK, D), BF16),
            shape((HD, SEQ), BF16),
            shape((CHUNK, 3 * HD), F32),
        ),
        in_specs=[
            SMEM_SPEC,
            VMEM_SPEC,
            VMEM_SPEC,
            HBM_SPEC,
            VMEM_SPEC,
            HBM_SPEC,
            VMEM_SPEC,
            VMEM_SPEC,
        ],
        out_specs=(VMEM_SPEC,) * 3,
        scratch_shapes=[
            pltpu.VMEM((D, 2 * ROWS), BF16),
            pltpu.VMEM((D, BLK), F32),
            pltpu.VMEM((D, BLK), F32),
            pltpu.VMEM((D, BLK), F32),
            pltpu.VMEM((D, SEQ), BF16),
            pltpu.VMEM((3, 2, 80, D), BF16),
            pltpu.SemaphoreType.DMA((3,)),
            pltpu.SemaphoreType.DMA((8,)),
        ],
        compiler_params=params(PREPARE_MB),
        cost_estimate=cost(5_000_000_000, 6_000_000),
        name="prepare",
    )(info, indices, table, normed_t, own_embedded, weights, hidden, out_t)


def backward_stage(
    info, inverse, mask, keys_head, values_head, queries_head, grads, slopes, weights
):
    return pl.pallas_call(
        backward_kernel,
        out_shape=(shape((4, BLK, 3 * HD), BF16), shape((NDP, 80, D), BF16)),
        in_specs=[SMEM_SPEC] * 3 + [VMEM_SPEC] * 5 + [HBM_SPEC],
        out_specs=(VMEM_SPEC, VMEM_SPEC),
        scratch_shapes=[pltpu.VMEM((CHUNK, HD), BF16)] * 3
        + [pltpu.VMEM((TILE, 3 * HD), F32), pltpu.SemaphoreType.DMA((4,))],
        compiler_params=params(43),
        name="backward",
    )(info, inverse, mask, keys_head, values_head, queries_head, grads, slopes, weights)


def core_stage(gate_grads, head_grads, weights, cotangent, own_embedded, own_terms, indices):
    return pl.pallas_call(
        core_kernel,
        out_shape=shape((2 * ROWS, D), BF16),
        in_specs=[VMEM_SPEC] * 7,
        out_specs=VMEM_SPEC,
        scratch_shapes=[
            pltpu.VMEM((D, BLK), F32),
            pltpu.VMEM((D, BLK), F32),
            pltpu.VMEM((D, 2 * BLK), F32),
        ],
        compiler_params=params(CORES_MB),
        name="cores",
    )(gate_grads, head_grads, weights, cotangent, own_embedded, own_terms, indices)


def pack_kernel(proj_t, out_t, packed):
    packed[:64, :] = proj_t[...]
    packed[64:, :E] = out_t[:16, :]
    packed[64:, E:] = out_t[16:, :]


def pack_weights(w_proj, w_out):
    return pl.pallas_call(
        pack_kernel,
        out_shape=shape((80, D), BF16),
        in_specs=[VMEM_SPEC] * 2,
        out_specs=VMEM_SPEC,
        compiler_params=params(60),
        name="pack",
    )(w_proj.T, w_out.T)


def pack_indices(item_first, item_second, block_mask):
    mask_row = jnp.pad(block_mask[0], ((0, 0), (0, BLK - NBLK)))
    return jnp.concatenate(
        [item_first, item_second, mask_row, jnp.zeros((5, BLK), jnp.int32)], axis=0
    )


def spread(values, axis, count):
    copies = jnp.broadcast_to(values[None], (count,) + values.shape)
    return lax.all_to_all(copies, axis, 0, 0)


def local(
    item_first, item_second, lengths, block_mask, core_first, core_second, w_proj, w_out, cotangent
):
    me = lax.axis_index("ctx").astype(jnp.int32)
    weights = lax.all_gather(pack_weights(w_proj, w_out), "dp", axis=0, tiled=True)
    weights = weights.reshape(NDP, 80, D)
    table = spread(jnp.concatenate([core_first, core_second], axis=0), "dp", NDP)
    table = table.reshape(2 * ROWS, D)
    own_indices = pack_indices(item_first, item_second, block_mask)
    indices = spread(own_indices, "ctx", NBLK)
    mask = indices[:, 2, :NBLK]
    info = jnp.stack([me, lengths[0, 0], lengths[0, 1], me])
    inverse = 1.0 / lengths[0].astype(F32)
    upstream = cotangent[0]

    normed_t, own_terms, own_embedded = embed_stage(info, indices, table)
    grads, gate_grads, hidden, keys_head, values_head, out_t = forward_stage(
        info, inverse, mask, normed_t, weights, upstream
    )
    grads = lax.all_to_all(grads, "ctx", 0, 0).reshape(SEQ, HD)
    layer_out, queries_head, slopes = prepare_stage(
        info, indices, table, normed_t, own_embedded, weights, hidden, out_t
    )
    pre_grads, weights_near = backward_stage(
        info, inverse, mask, keys_head, values_head, queries_head, grads, slopes, weights
    )
    groups = [[4 * c + h for h in range(4)] for c in range(4)]
    head_grads = lax.all_to_all(pre_grads, "ctx", 0, 0, axis_index_groups=groups)
    partial = core_stage(
        gate_grads, head_grads, weights_near, upstream, own_embedded, own_terms, own_indices
    )
    received = lax.all_to_all(partial.reshape(NDP, 8, D), "dp", 0, 0)
    pair_sum = jnp.sum(received.astype(F32), axis=0).astype(BF16)
    total = jnp.sum(spread(pair_sum, "ctx", NBLK).astype(F32), axis=0)
    return (layer_out[None], total[:4], total[4:])


def solution(mesh):
    placed = (
        P("dp", "ctx"),
        P("dp", "ctx"),
        P("dp", None),
        P("dp", "ctx", None),
        P("dp", None),
        P("dp", None),
        P(None, "dp"),
        P(None, "dp"),
        P("dp", "ctx", None),
    )
    return jax.shard_map(
        local,
        mesh=mesh,
        in_specs=placed,
        out_specs=(P("dp", "ctx", None), P("dp", None), P("dp", None)),
        check_vma=False,
    )
```

```python
import jax
import jax.numpy as jnp
from jax import lax
from jax.experimental import pallas as pl
from jax.experimental.pallas import tpu as pltpu
from jax.sharding import PartitionSpec as P

DA = 32
DB = 32
D = 1024
R = 32
ROWS = 128
H = 4
HD = 128
E = 512
BLK = 128
SEQ = 2048
NBLK = 16
TILE = 256
NDP = 32
CHUNK = 512
WIDE = 8
FORWARD_MB = 56
PREPARE_MB = 50
CORES_MB = 20

EPSILON = 1e-05
SCALE = HD ** (-0.5)
F32 = jnp.float32
BF16 = jnp.bfloat16
NT_DIMS = (((1,), (1,)), ((), ()))

SMEM_SPEC = pl.BlockSpec(memory_space=pltpu.SMEM)
VMEM_SPEC = pl.BlockSpec(memory_space=pltpu.VMEM)
HBM_SPEC = pl.BlockSpec(memory_space=pltpu.HBM)


def mm(left, right):
    return jnp.dot(left, right, preferred_element_type=F32)


def mm_nt(left, right):
    return lax.dot_general(left, right, NT_DIMS, preferred_element_type=F32)


def sigmoid(values):
    return 0.5 * jnp.tanh(0.5 * values) + 0.5


def silu(values):
    return values * sigmoid(values)


def silu_slope(values):
    sig = sigmoid(values)
    return sig * (1.0 + values * (1.0 - sig))


def flip(values):
    return values.astype(F32).T


def normalize(values, axis):
    average = jnp.mean(values, axis=axis, keepdims=True)
    centred = values - average
    inv_scale = lax.rsqrt(jnp.mean(centred * centred, axis=axis, keepdims=True) + EPSILON)
    return (centred * inv_scale, inv_scale)


def norm_back(upstream, normed, inv_scale):
    return (
        upstream
        - jnp.mean(upstream, axis=-1, keepdims=True)
        - normed * jnp.mean(upstream * normed, axis=-1, keepdims=True)
    ) * inv_scale


def pair_onehot(firsts, seconds):
    row = lax.broadcasted_iota(jnp.int32, (2 * ROWS, BLK), 0)
    core_row = ((row >> 3) << 2) | (row & 3)
    of_first = (row & 4) == 0
    hot_first = jnp.where(of_first & (core_row == firsts), 1.0, 0.0)
    hot_second = jnp.where((~of_first) & (core_row == seconds), 1.0, 0.0)
    return jnp.concatenate([hot_first, hot_second], axis=1).astype(BF16)


def aligned(index, unit):
    return pl.multiple_of(index * unit, unit)


def user_end(last_pos, first_len):
    return jnp.where(last_pos < first_len, first_len, SEQ)


def user_start(first_pos, first_len):
    return jnp.where(first_pos < first_len, 0, first_len)


def up_tiles(pos):
    return (pos + (TILE - 1)) // TILE


def block_range(chunk, first_len):
    low = (user_start(chunk * CHUNK, first_len) // TILE) * 2
    high = up_tiles(user_end(chunk * CHUNK + CHUNK - 1, first_len)) * 2
    return low, jnp.maximum(low, high - 12), high


def turn_table(table, table_t):
    for part in range(8):
        table_t[part * 128 : (part + 1) * 128, :] = flip(
            table[:, part * 128 : (part + 1) * 128]
        ).astype(BF16)


def embed_block(indices, position, table_t, rows_first, rows_second, emb):
    hot = pair_onehot(indices[position, 0:1, :], indices[position, 1:2, :])
    picked = mm(table_t[...], hot)
    rows_first[...] = picked[:, :BLK]
    rows_second[...] = picked[:, BLK:]

    def group(step, inner):
        base = aligned(step, WIDE * 32)
        sums = [jnp.zeros((DB, BLK), F32) for _ in range(WIDE)]
        for r in range(R):
            second = rows_second[r * DB : (r + 1) * DB, :]
            for k in range(WIDE):
                first = rows_first[pl.ds(base + (k * R + r), 1), :]
                sums[k] = sums[k] + first * second
        for k in range(WIDE):
            emb[pl.ds(pl.multiple_of(base + k * DB, DB), DB), :] = sums[k]
        return inner

    lax.fori_loop(0, DA // WIDE, group, 0)
    rounded = emb[...].astype(BF16)
    normed, unused = normalize(rounded.astype(F32), 0)
    return rounded, normed.astype(BF16)


def embed_kernel(
    info,
    indices,
    table,
    normed_far,
    own_terms,
    own_embedded,
    table_t,
    rows_first,
    rows_second,
    emb,
    normed_t,
    semaphores,
):
    me = info[0]
    unused, middle, high = block_range(me // 4, info[1])
    turn_table(table, table_t)

    def send(position):
        columns = pl.ds(aligned(position, BLK), BLK)
        return pltpu.make_async_copy(
            normed_t.at[:, columns], normed_far.at[:, columns], semaphores.at[position]
        )

    def block(position, carry):
        rounded, normed = embed_block(indices, position, table_t, rows_first, rows_second, emb)
        normed_t[:, pl.ds(aligned(position, BLK), BLK)] = normed
        send(position).start()

        @pl.when(position == me)
        def _():
            own_terms[0] = rows_first[...]
            own_terms[1] = rows_second[...]
            own_embedded[...] = rounded

        return carry

    def finish(position, carry):
        send(position).wait()
        return carry

    lax.fori_loop(middle, high, block, 0)
    lax.fori_loop(middle, high, finish, 0)


def weight_rows(weights, block, first=0, count=8):
    return weights[block * 8 + first : block * 8 + first + count, 0:64, :].reshape(count * 64, D)


def tile_scaling(row_first, column_first, shape, row_is_query, first_len, inverse, keep_low, keep_high):
    rows = row_first + lax.broadcasted_iota(jnp.int32, shape, 0)
    columns = column_first + lax.broadcasted_iota(jnp.int32, shape, 1)
    half = lax.broadcasted_iota(jnp.int32, shape, 1) < BLK
    query, key = (rows, columns) if row_is_query else (columns, rows)
    query_user = (query >= first_len).astype(jnp.int32)
    key_user = (key >= first_len).astype(jnp.int32)
    allowed = jnp.where(half, keep_low, keep_high)
    keep = (key >= query) & (query_user == key_user) & (allowed == 1)
    return jnp.where(keep, jnp.where(query_user == 1, inverse[1], inverse[0]), 0.0)


def square_scaling(mask, row_tile, column_tile, first_len, inverse, row_is_query):
    dims = (TILE, TILE)
    rows = row_tile * TILE + lax.broadcasted_iota(jnp.int32, dims, 0)
    columns = column_tile * TILE + lax.broadcasted_iota(jnp.int32, dims, 1)
    row_half = lax.broadcasted_iota(jnp.int32, dims, 0) < BLK
    column_half = lax.broadcasted_iota(jnp.int32, dims, 1) < BLK

    def flag(row, column):
        row, column = row_tile * 2 + row, column_tile * 2 + column
        return mask[row, column] if row_is_query else mask[column, row]

    allowed = jnp.where(
        row_half,
        jnp.where(column_half, flag(0, 0), flag(0, 1)),
        jnp.where(column_half, flag(1, 0), flag(1, 1)),
    )
    query, key = (rows, columns) if row_is_query else (columns, rows)
    query_user = (query >= first_len).astype(jnp.int32)
    key_user = (key >= first_len).astype(jnp.int32)
    keep = (key >= query) & (query_user == key_user) & (allowed == 1)
    return jnp.where(keep, jnp.where(query_user == 1, inverse[1], inverse[0]), 0.0)


def fetch(source, target, semaphore):
    copy = pltpu.make_async_copy(source, target, semaphore)
    copy.start()
    return copy


def fetch_weights(far, near, semaphores, order):
    parts = [pl.ds(block * 8, 8) for block in order]
    return [
        fetch(far.at[part], near.at[part], semaphores.at[place])
        for place, part in enumerate(parts)
    ]


def tile_copy(far, near, semaphores, position):
    columns = pl.ds(aligned(position, TILE), TILE)
    return pltpu.make_async_copy(far.at[:, columns], near.at[:, columns], semaphores.at[position])


def forward_kernel(
    info,
    inverse,
    mask,
    normed_far,
    weights_far,
    cotangent,
    grads_out,
    gate_out,
    hidden_out,
    keys_far,
    values_far,
    out_far,
    keys_t,
    values_t,
    mixed,
    queries,
    weights,
    normed_t,
    out_t,
    semaphores,
    tile_semaphores,
    away,
):
    copies = fetch_weights(weights_far, weights, semaphores, (1, 3, 2, 0))
    me = info[0]
    first_len = info[1]
    chunk = me // 4
    head = me % 4
    kv_low = chunk * 2
    kv_high = up_tiles(user_end(chunk * CHUNK + CHUNK - 1, first_len))

    def begin(position, carry):
        tile_copy(normed_far, normed_t, tile_semaphores, position).start()
        return carry

    lax.fori_loop(kv_low, kv_high, begin, 0)
    copies[0].wait()
    copies[1].wait()

    def kv_tile(position, carry):
        columns = pl.ds(aligned(position, TILE), TILE)
        tile_copy(normed_far, normed_t, tile_semaphores, position).wait()
        piece = normed_t[:, columns]
        values_t[:, columns] = silu(mm(weight_rows(weights, 1), piece)).astype(BF16)
        keys_t[:, columns] = silu(mm(weight_rows(weights, 3), piece)).astype(BF16)
        return carry

    lax.fori_loop(kv_low, kv_high, kv_tile, 0)
    head_rows = pl.ds(aligned(head, HD), HD)
    leaving = [
        fetch(keys_t.at[head_rows, :], keys_far, away.at[0]),
        fetch(values_t.at[head_rows, :], values_far, away.at[1]),
    ]
    copies[2].wait()
    copies[3].wait()

    for owner in range(NDP):
        out_t[owner * 32 : owner * 32 + 16, :] = weights[owner, 64:80, :E]
        out_t[owner * 32 + 16 : owner * 32 + 32, :] = weights[owner, 64:80, E:]
    leaving.append(fetch(out_t, out_far, away.at[2]))

    own_normed = flip(normed_t[:, pl.ds(aligned(me, BLK), BLK)]).astype(BF16)
    pre_gate = mm_nt(own_normed, weight_rows(weights, 0))
    gate = silu(pre_gate).astype(BF16).astype(F32)
    queries[...] = silu(mm_nt(own_normed, weight_rows(weights, 2))).astype(BF16)
    mixed[...] = jnp.zeros((BLK, E), F32)

    def attend(position, carry):
        columns = pl.ds(aligned(position, TILE), TILE)
        scaling = tile_scaling(
            me * BLK,
            position * TILE,
            (BLK, TILE),
            True,
            first_len,
            inverse,
            mask[me, position * 2],
            mask[me, position * 2 + 1],
        )
        for h in range(H):
            own = slice(h * HD, (h + 1) * HD)
            scores = mm(queries[:, own], keys_t[own, columns]) * SCALE
            attention = (silu(scores) * scaling).astype(BF16)
            mixed[:, own] += mm_nt(attention, values_t[own, columns])
        return carry

    lax.fori_loop(me // 2, up_tiles(user_end(me * BLK + BLK - 1, first_len)), attend, 0)

    hidden_grad = mm(cotangent[...], out_t[...])
    mixed_normed, mixed_scale = normalize(mixed[...], -1)
    mixed_grad = norm_back(hidden_grad * gate, mixed_normed, mixed_scale).astype(BF16)
    for place in range(NBLK):
        h = place % 4
        grads_out[place] = mixed_grad[:, h * HD : (h + 1) * HD]
    hidden_out[...] = (mixed_normed * gate).astype(BF16)
    gate_out[...] = (hidden_grad * mixed_normed * silu_slope(pre_gate)).astype(BF16)
    for copy in leaving:
        copy.wait()


def prepare_kernel(
    info,
    indices,
    table,
    normed_far,
    own_embedded,
    weights_far,
    hidden,
    out_t,
    layer_out,
    queries_head,
    slopes_out,
    table_t,
    rows_first,
    rows_second,
    emb,
    normed_t,
    head_weights,
    semaphores,
    tile_semaphores,
):
    me = info[0]
    first_len = info[1]
    chunk = me // 4
    head = me % 4
    copies = [
        fetch(
            weights_far.at[pl.ds(block * 8 + head * 2, 2)],
            head_weights.at[block - 1],
            semaphores.at[block - 1],
        )
        for block in (1, 2, 3)
    ]
    low, middle, unused = block_range(chunk, first_len)
    q_low = low // 2
    q_middle = jnp.minimum(middle, chunk * 4) // 2
    q_high = chunk * 2 + 2

    def begin(position, carry):
        tile_copy(normed_far, normed_t, tile_semaphores, position).start()
        return carry

    def finish(position, carry):
        tile_copy(normed_far, normed_t, tile_semaphores, position).wait()
        return carry

    lax.fori_loop(q_middle, q_high, begin, 0)
    turn_table(table, table_t)

    def late_block(position, carry):
        unused, normed = embed_block(indices, position, table_t, rows_first, rows_second, emb)
        normed_t[:, pl.ds(aligned(position, BLK), BLK)] = normed
        return carry

    lax.fori_loop(low, q_middle * 2, late_block, 0)
    layer_out[...] = (flip(own_embedded[...]) + mm_nt(hidden[...], out_t[...])).astype(BF16)
    for copy in copies:
        copy.wait()
    lax.fori_loop(q_middle, q_high, finish, 0)

    def rows_of(place):
        return head_weights[place, :, 0:64, :].reshape(HD, D)

    def q_tile(position, carry):
        tile = pl.ds(aligned(position, TILE), TILE)
        queries_head[:, tile] = silu(mm(rows_of(1), normed_t[:, tile])).astype(BF16)
        return carry

    lax.fori_loop(q_low, q_high, q_tile, 0)
    chunk_piece = normed_t[:, pl.ds(aligned(chunk, CHUNK), CHUNK)]
    for place in range(3):
        slopes_out[:, place * HD : (place + 1) * HD] = silu_slope(
            mm(rows_of(place), chunk_piece)
        ).T


def backward_kernel(
    info,
    inverse,
    mask,
    keys_head,
    values_head,
    queries_head,
    grads,
    slopes,
    weights_far,
    pre_grads,
    weights,
    own_keys,
    own_values,
    own_queries,
    sums,
    semaphores,
):
    copies = fetch_weights(weights_far, weights, semaphores, (0, 1, 2, 3))
    me = info[0]
    first_len = info[1]
    chunk = me // 4
    columns = pl.ds(aligned(chunk, CHUNK), CHUNK)
    own_keys[...] = flip(keys_head[:, columns]).astype(BF16)
    own_values[...] = flip(values_head[:, columns]).astype(BF16)
    own_queries[...] = flip(queries_head[:, columns]).astype(BF16)
    for part in range(2):
        place = chunk * 2 + part
        rows = slice(part * TILE, (part + 1) * TILE)
        sums[...] = jnp.zeros((TILE, 3 * HD), F32)

        def query_side(position, carry):
            tile = pl.ds(aligned(position, TILE), TILE)
            scaling = square_scaling(mask, place, position, first_len, inverse, True)
            scores = mm(own_queries[rows, :], keys_head[:, tile]) * SCALE
            pressure = mm(grads[pl.ds(aligned(place, TILE), TILE), :], values_head[:, tile])
            score_grad = (pressure * silu_slope(scores) * scaling).astype(BF16)
            sums[:, HD : 2 * HD] += mm_nt(score_grad, keys_head[:, tile])
            return carry

        lax.fori_loop(
            place, up_tiles(user_end(place * TILE + TILE - 1, first_len)), query_side, 0
        )

        def key_side(position, carry):
            tile = pl.ds(aligned(position, TILE), TILE)
            scaling = square_scaling(mask, place, position, first_len, inverse, False)
            scores = mm(own_keys[rows, :], queries_head[:, tile]) * SCALE
            sig = sigmoid(scores)
            grad_tile = grads[tile, :]
            attention = (scores * sig * scaling).astype(BF16)
            pressure = mm_nt(own_values[rows, :], grad_tile)
            slope = sig * (1.0 + scores * (1.0 - sig))
            score_grad = (pressure * slope * scaling).astype(BF16)
            sums[:, :HD] += mm(attention, grad_tile)
            sums[:, 2 * HD :] += mm_nt(score_grad, queries_head[:, tile])
            return carry

        lax.fori_loop(user_start(place * TILE, first_len) // TILE, place + 1, key_side, 0)
        for half in range(2):
            near = slice(half * BLK, (half + 1) * BLK)
            far = slice(part * TILE + half * BLK, part * TILE + (half + 1) * BLK)
            block = part * 2 + half
            pre_grads[block, :, :HD] = (sums[near, :HD] * slopes[far, :HD]).astype(BF16)
            pre_grads[block, :, HD:] = (sums[near, HD:] * SCALE * slopes[far, HD:]).astype(BF16)
    for copy in copies:
        copy.wait()


def core_kernel(
    gate_grads,
    head_grads,
    weights,
    cotangent,
    own_embedded,
    own_terms,
    indices,
    partial_out,
    rows_second,
    grad_t,
    terms,
):
    x_normed, x_scale = normalize(flip(own_embedded[...]), -1)
    normed_grad = mm(gate_grads[...], weight_rows(weights, 0))
    for place in range(3):
        joined = jnp.concatenate(
            [head_grads[h, :, place * HD : (place + 1) * HD] for h in range(H)], axis=1
        )
        normed_grad = normed_grad + mm(joined, weight_rows(weights, place + 1))
    input_grad = cotangent[...].astype(F32) + norm_back(normed_grad, x_normed, x_scale)
    grad_t[...] = input_grad.T
    for b in range(DB):
        rows_second[b * R : (b + 1) * R, :] = own_terms.at[1][pl.ds(b, R, stride=DB), :]

    def group(step, carry):
        base = aligned(step, WIDE * 32)
        sums = [jnp.zeros((R, BLK), F32) for _ in range(WIDE)]
        for b in range(DB):
            second = rows_second[b * R : (b + 1) * R, :]
            for k in range(WIDE):
                sums[k] = sums[k] + grad_t[pl.ds(base + (k * DB + b), 1), :] * second
        for k in range(WIDE):
            terms[pl.ds(pl.multiple_of(base + k * R, R), R), :BLK] = sums[k]
        sums = [jnp.zeros((DB, BLK), F32) for _ in range(WIDE)]
        for a in range(DA):
            grad = grad_t[a * DB : (a + 1) * DB, :]
            for k in range(WIDE):
                first = own_terms[0, pl.ds(a * R + step * WIDE + k, 1), :]
                sums[k] = sums[k] + first * grad
        for k in range(WIDE):
            terms[pl.ds(pl.multiple_of(base + k * DB, DB), DB), BLK:] = sums[k]
        return carry

    lax.fori_loop(0, DA // WIDE, group, 0)
    hot = pair_onehot(indices[0:1, :], indices[1:2, :])
    whole = terms[...]
    upper = whole.astype(BF16)
    lower = (whole - upper.astype(F32)).astype(BF16)
    total = mm_nt(hot, upper) + mm_nt(hot, lower)
    partial_out[...] = total.astype(BF16)


def params(megabytes):
    return pltpu.CompilerParams(vmem_limit_bytes=megabytes * 1024 * 1024)


def shape(dims, kind):
    return jax.ShapeDtypeStruct(dims, kind)


def embed_stage(info, indices, table):
    return pl.pallas_call(
        embed_kernel,
        out_shape=(shape((D, SEQ), BF16), shape((2, D, BLK), F32), shape((D, BLK), BF16)),
        in_specs=[SMEM_SPEC, VMEM_SPEC, VMEM_SPEC],
        out_specs=(HBM_SPEC, VMEM_SPEC, VMEM_SPEC),
        scratch_shapes=[
            pltpu.VMEM((D, 2 * ROWS), BF16),
            pltpu.VMEM((D, BLK), F32),
            pltpu.VMEM((D, BLK), F32),
            pltpu.VMEM((D, BLK), F32),
            pltpu.VMEM((D, SEQ), BF16),
            pltpu.SemaphoreType.DMA((NBLK,)),
        ],
        compiler_params=params(57),
        cost_estimate=pl.CostEstimate(flops=20_000_000_000, bytes_accessed=6_000_000, transcendentals=0),
        name="embed",
    )(info, indices, table)


def cost(flops, moved):
    return pl.CostEstimate(flops=flops, bytes_accessed=moved, transcendentals=0)


def forward_stage(info, inverse, mask, normed_t, weights, cotangent):
    return pl.pallas_call(
        forward_kernel,
        out_shape=(
            shape((NBLK, BLK, HD), BF16),
            shape((BLK, E), BF16),
            shape((BLK, E), BF16),
            shape((HD, SEQ), BF16),
            shape((HD, SEQ), BF16),
            shape((D, E), BF16),
        ),
        in_specs=[SMEM_SPEC] * 3 + [HBM_SPEC, HBM_SPEC, VMEM_SPEC],
        out_specs=(VMEM_SPEC,) * 3 + (HBM_SPEC,) * 3,
        scratch_shapes=[
            pltpu.VMEM((E, SEQ), BF16),
            pltpu.VMEM((E, SEQ), BF16),
            pltpu.VMEM((BLK, E), F32),
            pltpu.VMEM((BLK, E), BF16),
            pltpu.VMEM((NDP, 80, D), BF16),
            pltpu.VMEM((D, SEQ), BF16),
            pltpu.VMEM((D, E), BF16),
            pltpu.SemaphoreType.DMA((4,)),
            pltpu.SemaphoreType.DMA((8,)),
            pltpu.SemaphoreType.DMA((3,)),
        ],
        compiler_params=params(FORWARD_MB),
        cost_estimate=cost(8_000_000_000, 12_000_000),
        name="forward",
    )(info, inverse, mask, normed_t, weights, cotangent)


def prepare_stage(info, indices, table, normed_t, own_embedded, weights, hidden, out_t):
    return pl.pallas_call(
        prepare_kernel,
        out_shape=(
            shape((BLK, D), BF16),
            shape((HD, SEQ), BF16),
            shape((CHUNK, 3 * HD), F32),
        ),
        in_specs=[
            SMEM_SPEC,
            VMEM_SPEC,
            VMEM_SPEC,
            HBM_SPEC,
            VMEM_SPEC,
            HBM_SPEC,
            VMEM_SPEC,
            VMEM_SPEC,
        ],
        out_specs=(VMEM_SPEC,) * 3,
        scratch_shapes=[
            pltpu.VMEM((D, 2 * ROWS), BF16),
            pltpu.VMEM((D, BLK), F32),
            pltpu.VMEM((D, BLK), F32),
            pltpu.VMEM((D, BLK), F32),
            pltpu.VMEM((D, SEQ), BF16),
            pltpu.VMEM((3, 2, 80, D), BF16),
            pltpu.SemaphoreType.DMA((3,)),
            pltpu.SemaphoreType.DMA((8,)),
        ],
        compiler_params=params(PREPARE_MB),
        cost_estimate=cost(5_000_000_000, 6_000_000),
        name="prepare",
    )(info, indices, table, normed_t, own_embedded, weights, hidden, out_t)


def backward_stage(
    info, inverse, mask, keys_head, values_head, queries_head, grads, slopes, weights
):
    return pl.pallas_call(
        backward_kernel,
        out_shape=(shape((4, BLK, 3 * HD), BF16), shape((NDP, 80, D), BF16)),
        in_specs=[SMEM_SPEC] * 3 + [VMEM_SPEC] * 5 + [HBM_SPEC],
        out_specs=(VMEM_SPEC, VMEM_SPEC),
        scratch_shapes=[pltpu.VMEM((CHUNK, HD), BF16)] * 3
        + [pltpu.VMEM((TILE, 3 * HD), F32), pltpu.SemaphoreType.DMA((4,))],
        compiler_params=params(43),
        name="backward",
    )(info, inverse, mask, keys_head, values_head, queries_head, grads, slopes, weights)


def core_stage(gate_grads, head_grads, weights, cotangent, own_embedded, own_terms, indices):
    return pl.pallas_call(
        core_kernel,
        out_shape=shape((2 * ROWS, D), BF16),
        in_specs=[VMEM_SPEC] * 7,
        out_specs=VMEM_SPEC,
        scratch_shapes=[
            pltpu.VMEM((D, BLK), F32),
            pltpu.VMEM((D, BLK), F32),
            pltpu.VMEM((D, 2 * BLK), F32),
        ],
        compiler_params=params(CORES_MB),
        name="cores",
    )(gate_grads, head_grads, weights, cotangent, own_embedded, own_terms, indices)


def pack_kernel(
    proj_t, out_t, firsts, seconds, mask_row, core_first, core_second, packed, indices, tables, own
):
    packed[:64, :] = proj_t[...]
    packed[64:, :E] = out_t[:16, :]
    packed[64:, E:] = out_t[16:, :]
    indices[...] = jnp.zeros((NBLK, 8, BLK), jnp.int32)
    table = jnp.concatenate([core_first[...], core_second[...]], axis=0)
    for place in range(NBLK):
        indices[place, 0:1, :] = firsts[...]
        indices[place, 1:2, :] = seconds[...]
        indices[place, 2:3, 0:NBLK] = mask_row[...]
    for place in range(NDP):
        tables[place] = table
    own[...] = indices[0]


def pack_stage(w_proj, w_out, item_first, item_second, block_mask, core_first, core_second):
    return pl.pallas_call(
        pack_kernel,
        out_shape=(
            shape((80, D), BF16),
            shape((NBLK, 8, BLK), jnp.int32),
            shape((NDP, 8, D), BF16),
            shape((8, BLK), jnp.int32),
        ),
        in_specs=[VMEM_SPEC] * 7,
        out_specs=(VMEM_SPEC,) * 4,
        compiler_params=params(60),
        name="pack",
    )(w_proj.T, w_out.T, item_first, item_second, block_mask[0], core_first, core_second)


def sum_kernel(received, copies):
    total = jnp.sum(received[...].astype(F32), axis=0).astype(BF16)
    for place in range(4):
        copies[place] = total


def sum_stage(received):
    return pl.pallas_call(
        sum_kernel,
        out_shape=shape((4, 8, D), BF16),
        in_specs=[VMEM_SPEC],
        out_specs=VMEM_SPEC,
        compiler_params=params(16),
        name="sum",
    )(received)


def last_kernel(received, grad_first, grad_second):
    total = jnp.sum(received[...].astype(F32), axis=0)
    grad_first[...] = total[:4]
    grad_second[...] = total[4:]


def last_stage(received):
    return pl.pallas_call(
        last_kernel,
        out_shape=(shape((4, D), F32), shape((4, D), F32)),
        in_specs=[VMEM_SPEC],
        out_specs=(VMEM_SPEC,) * 2,
        compiler_params=params(16),
        name="last",
    )(received)


NEAR = [[4 * c + h for h in range(4)] for c in range(4)]
FAR = [[4 * c + h for c in range(4)] for h in range(4)]


def exchange(values, axis, groups=None):
    return lax.all_to_all(values, axis, 0, 0, axis_index_groups=groups)


def local(
    item_first, item_second, lengths, block_mask, core_first, core_second, w_proj, w_out, cotangent
):
    me = lax.axis_index("ctx").astype(jnp.int32)
    packed, index_copies, table_copies, own_indices = pack_stage(
        w_proj, w_out, item_first, item_second, block_mask, core_first, core_second
    )
    weights = lax.all_gather(packed, "dp", axis=0, tiled=True).reshape(NDP, 80, D)
    indices = exchange(index_copies, "ctx")
    table = exchange(table_copies, "dp").reshape(2 * ROWS, D)
    mask = indices[:, 2, :NBLK]
    info = jnp.stack([me, lengths[0, 0], lengths[0, 1], me])
    inverse = 1.0 / lengths[0].astype(F32)
    upstream = cotangent[0]

    normed_t, own_terms, own_embedded = embed_stage(info, indices, table)
    grads, gate_grads, hidden, keys_head, values_head, out_t = forward_stage(
        info, inverse, mask, normed_t, weights, upstream
    )
    grads = lax.all_to_all(grads, "ctx", 0, 0).reshape(SEQ, HD)
    layer_out, queries_head, slopes = prepare_stage(
        info, indices, table, normed_t, own_embedded, weights, hidden, out_t
    )
    pre_grads, weights_near = backward_stage(
        info, inverse, mask, keys_head, values_head, queries_head, grads, slopes, weights
    )
    head_grads = exchange(pre_grads, "ctx", NEAR)
    partial = core_stage(
        gate_grads, head_grads, weights_near, upstream, own_embedded, own_terms, own_indices
    )
    received = exchange(partial.reshape(NDP, 8, D), "dp")
    near_sum = exchange(sum_stage(received), "ctx", NEAR)
    grad_first, grad_second = last_stage(exchange(sum_stage(near_sum), "ctx", FAR))
    return (layer_out[None], grad_first, grad_second)


def solution(mesh):
    placed = (
        P("dp", "ctx"),
        P("dp", "ctx"),
        P("dp", None),
        P("dp", "ctx", None),
        P("dp", None),
        P("dp", None),
        P(None, "dp"),
        P(None, "dp"),
        P("dp", "ctx", None),
    )
    return jax.shard_map(
        local,
        mesh=mesh,
        in_specs=placed,
        out_specs=(P("dp", "ctx", None), P("dp", None), P("dp", None)),
        check_vma=False,
    )
```

```python
import jax
import jax.numpy as jnp
from jax import lax
from jax.experimental import pallas as pl
from jax.experimental.pallas import tpu as pltpu
from jax.sharding import PartitionSpec as P

DA = 32
DB = 32
D = 1024
R = 32
ROWS = 128
H = 4
HD = 128
E = 512
BLK = 128
SEQ = 2048
NBLK = 16
TILE = 256
NDP = 32
CHUNK = 512
WIDE = 8
FORWARD_MB = 56
PREPARE_MB = 50
CORES_MB = 20

EPSILON = 1e-05
SCALE = HD ** (-0.5)
F32 = jnp.float32
BF16 = jnp.bfloat16
NT_DIMS = (((1,), (1,)), ((), ()))

SMEM_SPEC = pl.BlockSpec(memory_space=pltpu.SMEM)
VMEM_SPEC = pl.BlockSpec(memory_space=pltpu.VMEM)
HBM_SPEC = pl.BlockSpec(memory_space=pltpu.HBM)


def mm(left, right):
    return jnp.dot(left, right, preferred_element_type=F32)


def mm_nt(left, right):
    return lax.dot_general(left, right, NT_DIMS, preferred_element_type=F32)


def sigmoid(values):
    return 0.5 * jnp.tanh(0.5 * values) + 0.5


def silu(values):
    return values * sigmoid(values)


def silu_slope(values):
    sig = sigmoid(values)
    return sig * (1.0 + values * (1.0 - sig))


def flip(values):
    return values.astype(F32).T


def normalize(values, axis):
    average = jnp.mean(values, axis=axis, keepdims=True)
    centred = values - average
    inv_scale = lax.rsqrt(jnp.mean(centred * centred, axis=axis, keepdims=True) + EPSILON)
    return (centred * inv_scale, inv_scale)


def norm_back(upstream, normed, inv_scale):
    return (
        upstream
        - jnp.mean(upstream, axis=-1, keepdims=True)
        - normed * jnp.mean(upstream * normed, axis=-1, keepdims=True)
    ) * inv_scale


def pair_onehot(firsts, seconds):
    row = lax.broadcasted_iota(jnp.int32, (2 * ROWS, BLK), 0)
    core_row = ((row >> 3) << 2) | (row & 3)
    of_first = (row & 4) == 0
    hot_first = jnp.where(of_first & (core_row == firsts), 1.0, 0.0)
    hot_second = jnp.where((~of_first) & (core_row == seconds), 1.0, 0.0)
    return jnp.concatenate([hot_first, hot_second], axis=1).astype(BF16)


def aligned(index, unit):
    return pl.multiple_of(index * unit, unit)


def user_end(last_pos, first_len):
    return jnp.where(last_pos < first_len, first_len, SEQ)


def user_start(first_pos, first_len):
    return jnp.where(first_pos < first_len, 0, first_len)


def up_tiles(pos):
    return (pos + (TILE - 1)) // TILE


def block_range(chunk, first_len):
    low = (user_start(chunk * CHUNK, first_len) // TILE) * 2
    high = up_tiles(user_end(chunk * CHUNK + CHUNK - 1, first_len)) * 2
    return low, jnp.maximum(low, high - 12), high


def turn_table(table, table_t):
    for part in range(8):
        table_t[part * 128 : (part + 1) * 128, :] = flip(
            table[:, part * 128 : (part + 1) * 128]
        ).astype(BF16)


def embed_block(indices, position, table_t, rows_first, rows_second, emb):
    hot = pair_onehot(indices[position, 0:1, :], indices[position, 1:2, :])
    picked = mm(table_t[...], hot)
    rows_first[...] = picked[:, :BLK]
    rows_second[...] = picked[:, BLK:]

    def group(step, inner):
        base = aligned(step, WIDE * 32)
        sums = [jnp.zeros((DB, BLK), F32) for _ in range(WIDE)]
        for r in range(R):
            second = rows_second[r * DB : (r + 1) * DB, :]
            for k in range(WIDE):
                first = rows_first[pl.ds(base + (k * R + r), 1), :]
                sums[k] = sums[k] + first * second
        for k in range(WIDE):
            emb[pl.ds(pl.multiple_of(base + k * DB, DB), DB), :] = sums[k]
        return inner

    lax.fori_loop(0, DA // WIDE, group, 0)
    rounded = emb[...].astype(BF16)
    normed, unused = normalize(rounded.astype(F32), 0)
    return rounded, normed.astype(BF16)


def embed_kernel(
    info,
    indices,
    table,
    normed_far,
    own_terms,
    own_embedded,
    table_t,
    rows_first,
    rows_second,
    emb,
    normed_t,
    semaphores,
):
    me = info[0]
    unused, middle, high = block_range(me // 4, info[1])
    turn_table(table, table_t)

    def send(position):
        columns = pl.ds(aligned(position, BLK), BLK)
        return pltpu.make_async_copy(
            normed_t.at[:, columns], normed_far.at[:, columns], semaphores.at[position]
        )

    def block(position, carry):
        rounded, normed = embed_block(indices, position, table_t, rows_first, rows_second, emb)
        normed_t[:, pl.ds(aligned(position, BLK), BLK)] = normed
        send(position).start()

        @pl.when(position == me)
        def _():
            own_terms[0] = rows_first[...]
            own_terms[1] = rows_second[...]
            own_embedded[...] = rounded

        return carry

    def finish(position, carry):
        send(position).wait()
        return carry

    lax.fori_loop(middle, high, block, 0)
    lax.fori_loop(middle, high, finish, 0)


def weight_rows(weights, block, first=0, count=8):
    return weights[block * 8 + first : block * 8 + first + count, 0:64, :].reshape(count * 64, D)


def tile_scaling(row_first, column_first, shape, row_is_query, first_len, inverse, keep_low, keep_high):
    rows = row_first + lax.broadcasted_iota(jnp.int32, shape, 0)
    columns = column_first + lax.broadcasted_iota(jnp.int32, shape, 1)
    half = lax.broadcasted_iota(jnp.int32, shape, 1) < BLK
    query, key = (rows, columns) if row_is_query else (columns, rows)
    query_user = (query >= first_len).astype(jnp.int32)
    key_user = (key >= first_len).astype(jnp.int32)
    allowed = jnp.where(half, keep_low, keep_high)
    keep = (key >= query) & (query_user == key_user) & (allowed == 1)
    return jnp.where(keep, jnp.where(query_user == 1, inverse[1], inverse[0]), 0.0)


def square_scaling(mask, row_tile, column_tile, first_len, inverse, row_is_query):
    dims = (TILE, TILE)
    rows = row_tile * TILE + lax.broadcasted_iota(jnp.int32, dims, 0)
    columns = column_tile * TILE + lax.broadcasted_iota(jnp.int32, dims, 1)
    row_half = lax.broadcasted_iota(jnp.int32, dims, 0) < BLK
    column_half = lax.broadcasted_iota(jnp.int32, dims, 1) < BLK

    def flag(row, column):
        row, column = row_tile * 2 + row, column_tile * 2 + column
        return mask[row, column] if row_is_query else mask[column, row]

    allowed = jnp.where(
        row_half,
        jnp.where(column_half, flag(0, 0), flag(0, 1)),
        jnp.where(column_half, flag(1, 0), flag(1, 1)),
    )
    query, key = (rows, columns) if row_is_query else (columns, rows)
    query_user = (query >= first_len).astype(jnp.int32)
    key_user = (key >= first_len).astype(jnp.int32)
    keep = (key >= query) & (query_user == key_user) & (allowed == 1)
    return jnp.where(keep, jnp.where(query_user == 1, inverse[1], inverse[0]), 0.0)


def fetch(source, target, semaphore):
    copy = pltpu.make_async_copy(source, target, semaphore)
    copy.start()
    return copy


def fetch_weights(far, near, semaphores, order):
    parts = [pl.ds(block * 8, 8) for block in order]
    return [
        fetch(far.at[part], near.at[part], semaphores.at[place])
        for place, part in enumerate(parts)
    ]


def tile_copy(far, near, semaphores, position):
    columns = pl.ds(aligned(position, TILE), TILE)
    return pltpu.make_async_copy(far.at[:, columns], near.at[:, columns], semaphores.at[position])


def forward_kernel(
    info,
    inverse,
    mask,
    normed_far,
    weights_far,
    cotangent,
    grads_out,
    gate_out,
    hidden_out,
    keys_far,
    values_far,
    out_far,
    keys_t,
    values_t,
    mixed,
    queries,
    weights,
    normed_t,
    out_t,
    semaphores,
    tile_semaphores,
    away,
):
    copies = fetch_weights(weights_far, weights, semaphores, (1, 3, 2, 0))
    me = info[0]
    first_len = info[1]
    chunk = me // 4
    head = me % 4
    kv_low = chunk * 2
    kv_high = up_tiles(user_end(chunk * CHUNK + CHUNK - 1, first_len))

    def begin(position, carry):
        tile_copy(normed_far, normed_t, tile_semaphores, position).start()
        return carry

    lax.fori_loop(kv_low, kv_high, begin, 0)
    copies[0].wait()
    copies[1].wait()

    def kv_tile(position, carry):
        columns = pl.ds(aligned(position, TILE), TILE)
        tile_copy(normed_far, normed_t, tile_semaphores, position).wait()
        piece = normed_t[:, columns]
        values_t[:, columns] = silu(mm(weight_rows(weights, 1), piece)).astype(BF16)
        keys_t[:, columns] = silu(mm(weight_rows(weights, 3), piece)).astype(BF16)
        return carry

    lax.fori_loop(kv_low, kv_high, kv_tile, 0)
    head_rows = pl.ds(aligned(head, HD), HD)
    leaving = [
        fetch(keys_t.at[head_rows, :], keys_far, away.at[0]),
        fetch(values_t.at[head_rows, :], values_far, away.at[1]),
    ]
    copies[2].wait()
    copies[3].wait()

    for owner in range(NDP):
        out_t[owner * 32 : owner * 32 + 16, :] = weights[owner, 64:80, :E]
        out_t[owner * 32 + 16 : owner * 32 + 32, :] = weights[owner, 64:80, E:]
    leaving.append(fetch(out_t, out_far, away.at[2]))

    own_normed = flip(normed_t[:, pl.ds(aligned(me, BLK), BLK)]).astype(BF16)
    pre_gate = mm_nt(own_normed, weight_rows(weights, 0))
    gate = silu(pre_gate).astype(BF16).astype(F32)
    queries[...] = silu(mm_nt(own_normed, weight_rows(weights, 2))).astype(BF16)
    mixed[...] = jnp.zeros((BLK, E), F32)

    def attend(position, carry):
        columns = pl.ds(aligned(position, TILE), TILE)
        scaling = tile_scaling(
            me * BLK,
            position * TILE,
            (BLK, TILE),
            True,
            first_len,
            inverse,
            mask[me, position * 2],
            mask[me, position * 2 + 1],
        )
        for h in range(H):
            own = slice(h * HD, (h + 1) * HD)
            scores = mm(queries[:, own], keys_t[own, columns]) * SCALE
            attention = (silu(scores) * scaling).astype(BF16)
            mixed[:, own] += mm_nt(attention, values_t[own, columns])
        return carry

    lax.fori_loop(me // 2, up_tiles(user_end(me * BLK + BLK - 1, first_len)), attend, 0)

    hidden_grad = mm(cotangent[...], out_t[...])
    mixed_normed, mixed_scale = normalize(mixed[...], -1)
    mixed_grad = norm_back(hidden_grad * gate, mixed_normed, mixed_scale).astype(BF16)
    for place in range(NBLK):
        h = place % 4
        grads_out[place] = mixed_grad[:, h * HD : (h + 1) * HD]
    hidden_out[...] = (mixed_normed * gate).astype(BF16)
    gate_out[...] = (hidden_grad * mixed_normed * silu_slope(pre_gate)).astype(BF16)
    for copy in leaving:
        copy.wait()


def prepare_kernel(
    info,
    indices,
    table,
    normed_far,
    own_embedded,
    weights_far,
    hidden,
    out_t,
    layer_out,
    queries_head,
    slopes_out,
    table_t,
    rows_first,
    rows_second,
    emb,
    normed_t,
    head_weights,
    semaphores,
    tile_semaphores,
):
    me = info[0]
    first_len = info[1]
    chunk = me // 4
    head = me % 4
    copies = [
        fetch(
            weights_far.at[pl.ds(block * 8 + head * 2, 2)],
            head_weights.at[block - 1],
            semaphores.at[block - 1],
        )
        for block in (1, 2, 3)
    ]
    low, middle, unused = block_range(chunk, first_len)
    q_low = low // 2
    q_middle = jnp.minimum(middle, chunk * 4) // 2
    q_high = chunk * 2 + 2

    def begin(position, carry):
        tile_copy(normed_far, normed_t, tile_semaphores, position).start()
        return carry

    def finish(position, carry):
        tile_copy(normed_far, normed_t, tile_semaphores, position).wait()
        return carry

    lax.fori_loop(q_middle, q_high, begin, 0)
    turn_table(table, table_t)

    def late_block(position, carry):
        unused, normed = embed_block(indices, position, table_t, rows_first, rows_second, emb)
        normed_t[:, pl.ds(aligned(position, BLK), BLK)] = normed
        return carry

    lax.fori_loop(low, q_middle * 2, late_block, 0)
    layer_out[...] = (flip(own_embedded[...]) + mm_nt(hidden[...], out_t[...])).astype(BF16)
    for copy in copies:
        copy.wait()
    lax.fori_loop(q_middle, q_high, finish, 0)

    def rows_of(place):
        return head_weights[place, :, 0:64, :].reshape(HD, D)

    def q_tile(position, carry):
        tile = pl.ds(aligned(position, TILE), TILE)
        queries_head[:, tile] = silu(mm(rows_of(1), normed_t[:, tile])).astype(BF16)
        return carry

    lax.fori_loop(q_low, q_high, q_tile, 0)
    chunk_piece = normed_t[:, pl.ds(aligned(chunk, CHUNK), CHUNK)]
    for place in range(3):
        slopes_out[:, place * HD : (place + 1) * HD] = silu_slope(
            mm(rows_of(place), chunk_piece)
        ).T


def backward_kernel(
    info,
    inverse,
    mask,
    keys_head,
    values_head,
    queries_head,
    grads,
    slopes,
    weights_far,
    pre_grads,
    weights,
    own_keys,
    own_values,
    own_queries,
    sums,
    semaphores,
):
    copies = fetch_weights(weights_far, weights, semaphores, (0, 1, 2, 3))
    me = info[0]
    first_len = info[1]
    chunk = me // 4
    columns = pl.ds(aligned(chunk, CHUNK), CHUNK)
    own_keys[...] = flip(keys_head[:, columns]).astype(BF16)
    own_values[...] = flip(values_head[:, columns]).astype(BF16)
    own_queries[...] = flip(queries_head[:, columns]).astype(BF16)
    for part in range(2):
        place = chunk * 2 + part
        rows = slice(part * TILE, (part + 1) * TILE)
        sums[...] = jnp.zeros((TILE, 3 * HD), F32)

        def query_side(position, carry):
            tile = pl.ds(aligned(position, TILE), TILE)
            scaling = square_scaling(mask, place, position, first_len, inverse, True)
            scores = mm(own_queries[rows, :], keys_head[:, tile]) * SCALE
            pressure = mm(grads[pl.ds(aligned(place, TILE), TILE), :], values_head[:, tile])
            score_grad = (pressure * silu_slope(scores) * scaling).astype(BF16)
            sums[:, HD : 2 * HD] += mm_nt(score_grad, keys_head[:, tile])
            return carry

        lax.fori_loop(
            place, up_tiles(user_end(place * TILE + TILE - 1, first_len)), query_side, 0
        )

        def key_side(position, carry):
            tile = pl.ds(aligned(position, TILE), TILE)
            scaling = square_scaling(mask, place, position, first_len, inverse, False)
            scores = mm(own_keys[rows, :], queries_head[:, tile]) * SCALE
            sig = sigmoid(scores)
            grad_tile = grads[tile, :]
            attention = (scores * sig * scaling).astype(BF16)
            pressure = mm_nt(own_values[rows, :], grad_tile)
            slope = sig * (1.0 + scores * (1.0 - sig))
            score_grad = (pressure * slope * scaling).astype(BF16)
            sums[:, :HD] += mm(attention, grad_tile)
            sums[:, 2 * HD :] += mm_nt(score_grad, queries_head[:, tile])
            return carry

        lax.fori_loop(user_start(place * TILE, first_len) // TILE, place + 1, key_side, 0)
        for half in range(2):
            near = slice(half * BLK, (half + 1) * BLK)
            far = slice(part * TILE + half * BLK, part * TILE + (half + 1) * BLK)
            block = part * 2 + half
            pre_grads[block, :, :HD] = (sums[near, :HD] * slopes[far, :HD]).astype(BF16)
            pre_grads[block, :, HD:] = (sums[near, HD:] * SCALE * slopes[far, HD:]).astype(BF16)
    for copy in copies:
        copy.wait()


def core_kernel(
    gate_grads,
    head_grads,
    weights,
    cotangent,
    own_embedded,
    own_terms,
    indices,
    partial_out,
    rows_second,
    grad_t,
    terms,
):
    x_normed, x_scale = normalize(flip(own_embedded[...]), -1)
    normed_grad = mm(gate_grads[...], weight_rows(weights, 0))
    for place in range(3):
        joined = jnp.concatenate(
            [head_grads[h, :, place * HD : (place + 1) * HD] for h in range(H)], axis=1
        )
        normed_grad = normed_grad + mm(joined, weight_rows(weights, place + 1))
    input_grad = cotangent[...].astype(F32) + norm_back(normed_grad, x_normed, x_scale)
    grad_t[...] = input_grad.T
    for b in range(DB):
        rows_second[b * R : (b + 1) * R, :] = own_terms.at[1][pl.ds(b, R, stride=DB), :]

    def group(step, carry):
        base = aligned(step, WIDE * 32)
        sums = [jnp.zeros((R, BLK), F32) for _ in range(WIDE)]
        for b in range(DB):
            second = rows_second[b * R : (b + 1) * R, :]
            for k in range(WIDE):
                sums[k] = sums[k] + grad_t[pl.ds(base + (k * DB + b), 1), :] * second
        for k in range(WIDE):
            terms[pl.ds(pl.multiple_of(base + k * R, R), R), :BLK] = sums[k]
        sums = [jnp.zeros((DB, BLK), F32) for _ in range(WIDE)]
        for a in range(DA):
            grad = grad_t[a * DB : (a + 1) * DB, :]
            for k in range(WIDE):
                first = own_terms[0, pl.ds(a * R + step * WIDE + k, 1), :]
                sums[k] = sums[k] + first * grad
        for k in range(WIDE):
            terms[pl.ds(pl.multiple_of(base + k * DB, DB), DB), BLK:] = sums[k]
        return carry

    lax.fori_loop(0, DA // WIDE, group, 0)
    hot = pair_onehot(indices[0:1, :], indices[1:2, :])
    whole = terms[...]
    upper = whole.astype(BF16)
    lower = (whole - upper.astype(F32)).astype(BF16)
    total = mm_nt(hot, upper) + mm_nt(hot, lower)
    partial_out[...] = total.astype(BF16)


def params(megabytes):
    return pltpu.CompilerParams(vmem_limit_bytes=megabytes * 1024 * 1024)


def shape(dims, kind):
    return jax.ShapeDtypeStruct(dims, kind)


def embed_stage(info, indices, table):
    return pl.pallas_call(
        embed_kernel,
        out_shape=(shape((D, SEQ), BF16), shape((2, D, BLK), F32), shape((D, BLK), BF16)),
        in_specs=[SMEM_SPEC, VMEM_SPEC, VMEM_SPEC],
        out_specs=(HBM_SPEC, VMEM_SPEC, VMEM_SPEC),
        scratch_shapes=[
            pltpu.VMEM((D, 2 * ROWS), BF16),
            pltpu.VMEM((D, BLK), F32),
            pltpu.VMEM((D, BLK), F32),
            pltpu.VMEM((D, BLK), F32),
            pltpu.VMEM((D, SEQ), BF16),
            pltpu.SemaphoreType.DMA((NBLK,)),
        ],
        compiler_params=params(57),
        cost_estimate=pl.CostEstimate(flops=20_000_000_000, bytes_accessed=6_000_000, transcendentals=0),
        name="embed",
    )(info, indices, table)


def cost(flops, moved):
    return pl.CostEstimate(flops=flops, bytes_accessed=moved, transcendentals=0)


def forward_stage(info, inverse, mask, normed_t, weights, cotangent):
    return pl.pallas_call(
        forward_kernel,
        out_shape=(
            shape((NBLK, BLK, HD), BF16),
            shape((BLK, E), BF16),
            shape((BLK, E), BF16),
            shape((HD, SEQ), BF16),
            shape((HD, SEQ), BF16),
            shape((D, E), BF16),
        ),
        in_specs=[SMEM_SPEC] * 3 + [HBM_SPEC, HBM_SPEC, VMEM_SPEC],
        out_specs=(VMEM_SPEC,) * 3 + (HBM_SPEC,) * 3,
        scratch_shapes=[
            pltpu.VMEM((E, SEQ), BF16),
            pltpu.VMEM((E, SEQ), BF16),
            pltpu.VMEM((BLK, E), F32),
            pltpu.VMEM((BLK, E), BF16),
            pltpu.VMEM((NDP, 80, D), BF16),
            pltpu.VMEM((D, SEQ), BF16),
            pltpu.VMEM((D, E), BF16),
            pltpu.SemaphoreType.DMA((4,)),
            pltpu.SemaphoreType.DMA((8,)),
            pltpu.SemaphoreType.DMA((3,)),
        ],
        compiler_params=params(FORWARD_MB),
        cost_estimate=cost(8_000_000_000, 12_000_000),
        name="forward",
    )(info, inverse, mask, normed_t, weights, cotangent)


def prepare_stage(info, indices, table, normed_t, own_embedded, weights, hidden, out_t):
    return pl.pallas_call(
        prepare_kernel,
        out_shape=(
            shape((BLK, D), BF16),
            shape((HD, SEQ), BF16),
            shape((CHUNK, 3 * HD), F32),
        ),
        in_specs=[
            SMEM_SPEC,
            VMEM_SPEC,
            VMEM_SPEC,
            HBM_SPEC,
            VMEM_SPEC,
            HBM_SPEC,
            VMEM_SPEC,
            VMEM_SPEC,
        ],
        out_specs=(VMEM_SPEC,) * 3,
        scratch_shapes=[
            pltpu.VMEM((D, 2 * ROWS), BF16),
            pltpu.VMEM((D, BLK), F32),
            pltpu.VMEM((D, BLK), F32),
            pltpu.VMEM((D, BLK), F32),
            pltpu.VMEM((D, SEQ), BF16),
            pltpu.VMEM((3, 2, 80, D), BF16),
            pltpu.SemaphoreType.DMA((3,)),
            pltpu.SemaphoreType.DMA((8,)),
        ],
        compiler_params=params(PREPARE_MB),
        cost_estimate=cost(5_000_000_000, 6_000_000),
        name="prepare",
    )(info, indices, table, normed_t, own_embedded, weights, hidden, out_t)


def backward_stage(
    info, inverse, mask, keys_head, values_head, queries_head, grads, slopes, weights
):
    return pl.pallas_call(
        backward_kernel,
        out_shape=(shape((4, BLK, 3 * HD), BF16), shape((NDP, 80, D), BF16)),
        in_specs=[SMEM_SPEC] * 3 + [VMEM_SPEC] * 5 + [HBM_SPEC],
        out_specs=(VMEM_SPEC, VMEM_SPEC),
        scratch_shapes=[pltpu.VMEM((CHUNK, HD), BF16)] * 3
        + [pltpu.VMEM((TILE, 3 * HD), F32), pltpu.SemaphoreType.DMA((4,))],
        compiler_params=params(43),
        name="backward",
    )(info, inverse, mask, keys_head, values_head, queries_head, grads, slopes, weights)


def core_stage(gate_grads, head_grads, weights, cotangent, own_embedded, own_terms, indices):
    return pl.pallas_call(
        core_kernel,
        out_shape=shape((2 * ROWS, D), BF16),
        in_specs=[VMEM_SPEC] * 7,
        out_specs=VMEM_SPEC,
        scratch_shapes=[
            pltpu.VMEM((D, BLK), F32),
            pltpu.VMEM((D, BLK), F32),
            pltpu.VMEM((D, 2 * BLK), F32),
        ],
        compiler_params=params(CORES_MB),
        name="cores",
    )(gate_grads, head_grads, weights, cotangent, own_embedded, own_terms, indices)


def pack_kernel(
    proj_t, out_t, firsts, seconds, mask_row, core_first, core_second, packed, indices, tables, own
):
    packed[:64, :] = proj_t[...]
    packed[64:, :E] = out_t[:16, :]
    packed[64:, E:] = out_t[16:, :]
    indices[...] = jnp.zeros((NBLK, 8, BLK), jnp.int32)
    table = jnp.concatenate([core_first[...], core_second[...]], axis=0)
    for place in range(NBLK):
        indices[place, 0:1, :] = firsts[...]
        indices[place, 1:2, :] = seconds[...]
        indices[place, 2:3, 0:NBLK] = mask_row[...]
    for place in range(NDP):
        tables[place] = table
    own[...] = indices[0]


def pack_stage(w_proj, w_out, item_first, item_second, block_mask, core_first, core_second):
    return pl.pallas_call(
        pack_kernel,
        out_shape=(
            shape((80, D), BF16),
            shape((NBLK, 8, BLK), jnp.int32),
            shape((NDP, 8, D), BF16),
            shape((8, BLK), jnp.int32),
        ),
        in_specs=[VMEM_SPEC] * 7,
        out_specs=(VMEM_SPEC,) * 4,
        compiler_params=params(60),
        name="pack",
    )(w_proj.T, w_out.T, item_first, item_second, block_mask[0], core_first, core_second)


def sum_kernel(received, copies):
    total = jnp.sum(received[...].astype(F32), axis=0).astype(BF16)
    for place in range(NBLK):
        copies[place] = total


def sum_stage(received):
    return pl.pallas_call(
        sum_kernel,
        out_shape=shape((NBLK, 8, D), BF16),
        in_specs=[VMEM_SPEC],
        out_specs=VMEM_SPEC,
        compiler_params=params(16),
        name="sum",
    )(received)


def last_kernel(received, grad_first, grad_second):
    total = jnp.sum(received[...].astype(F32), axis=0)
    grad_first[...] = total[:4]
    grad_second[...] = total[4:]


def last_stage(received):
    return pl.pallas_call(
        last_kernel,
        out_shape=(shape((4, D), F32), shape((4, D), F32)),
        in_specs=[VMEM_SPEC],
        out_specs=(VMEM_SPEC,) * 2,
        compiler_params=params(16),
        name="last",
    )(received)


NEAR = [[4 * c + h for h in range(4)] for c in range(4)]


def exchange(values, axis, groups=None):
    return lax.all_to_all(values, axis, 0, 0, axis_index_groups=groups)


def local(
    item_first, item_second, lengths, block_mask, core_first, core_second, w_proj, w_out, cotangent
):
    me = lax.axis_index("ctx").astype(jnp.int32)
    packed, index_copies, table_copies, own_indices = pack_stage(
        w_proj, w_out, item_first, item_second, block_mask, core_first, core_second
    )
    weights = lax.all_gather(packed, "dp", axis=0, tiled=True).reshape(NDP, 80, D)
    indices = exchange(index_copies, "ctx")
    table = exchange(table_copies, "dp").reshape(2 * ROWS, D)
    mask = indices[:, 2, :NBLK]
    info = jnp.stack([me, lengths[0, 0], lengths[0, 1], me])
    inverse = 1.0 / lengths[0].astype(F32)
    upstream = cotangent[0]

    normed_t, own_terms, own_embedded = embed_stage(info, indices, table)
    grads, gate_grads, hidden, keys_head, values_head, out_t = forward_stage(
        info, inverse, mask, normed_t, weights, upstream
    )
    grads = lax.all_to_all(grads, "ctx", 0, 0).reshape(SEQ, HD)
    layer_out, queries_head, slopes = prepare_stage(
        info, indices, table, normed_t, own_embedded, weights, hidden, out_t
    )
    pre_grads, weights_near = backward_stage(
        info, inverse, mask, keys_head, values_head, queries_head, grads, slopes, weights
    )
    head_grads = exchange(pre_grads, "ctx", NEAR)
    partial = core_stage(
        gate_grads, head_grads, weights_near, upstream, own_embedded, own_terms, own_indices
    )
    received = exchange(partial.reshape(NDP, 8, D), "dp")
    grad_first, grad_second = last_stage(exchange(sum_stage(received), "ctx"))
    return (layer_out[None], grad_first, grad_second)


def solution(mesh):
    placed = (
        P("dp", "ctx"),
        P("dp", "ctx"),
        P("dp", None),
        P("dp", "ctx", None),
        P("dp", None),
        P("dp", None),
        P(None, "dp"),
        P(None, "dp"),
        P("dp", "ctx", None),
    )
    return jax.shard_map(
        local,
        mesh=mesh,
        in_specs=placed,
        out_specs=(P("dp", "ctx", None), P("dp", None), P("dp", None)),
        check_vma=False,
    )
```
